256 devices in a mesh: grp: 8 (over z_lo, core), row: 32 (over y, z_hi, x).
Axes of the slice: x: 4, y: 4, z: 8 (z_hi: 2, z_lo: 4; z = z_hi * 4 + z_lo), core: 2. Of those that a mesh axis runs over, the one named last changes fastest.
Arguments:
- coefficients: float32 [2, 24576, 1024], P(None, 'row', 'grp'), may hold values from -6 to 6
- hamiltonian: bfloat16 [384, 12, 64, 128], P('row'), may hold values from -0.15625 to 0.15625
- neighbours: int32 [384, 12], P('row'), may hold values from 0 to 383, as said below
- positions: float32 [3, 384], replicated, may hold values from -4 to 4
- atom_site: int32 [384], replicated, may hold values from 0 to 16383
- rs_field: float32 [6, 256, 128, 128], P(None, ('grp', 'row')), may hold values from -6 to 6
- potential: float32 [3, 256, 128, 128], P(None, ('grp', 'row')), may hold values from -6 to 6
Outputs:
- coefficients_out: float32 [2, 24576, 1024], P(None, 'row', 'grp')
- field_out: float32 [6, 256, 128, 128], P(None, ('grp', 'row'))
- potential_out: float32 [3, 256, 128, 128], P(None, ('grp', 'row'))
The draws below stay inside these ranges and needn't reach their ends.
Inputs may be any that keep to these rules, and one draw needn't show every extreme that they name: `neighbours`: each row's first block is the cluster itself, the second and third the clusters 6 after and 6 before it (a cluster beyond an end of the list is replaced by its mirror, the cluster as far on the other side); the others lie within 6 clusters of the row and may repeat. Every entry lies within 6 clusters of its row.
All inputs are finite; a program needn't handle non-finite values.
Results may differ from the reference program's by a relative error of at most 0.005.
Values may be sent and summed in bfloat16 or wider, within the bound.
A program may use at most 128 MiB of HBM per device.

```python
import math
import jax
import jax.numpy as jnp
from jax import lax

ORB = 64
NB = 12
ATOM_DEV = 12
TERMS = 3
STEPS = 1
GY = 128
GZ = 128
ATOMS = 384
ORBS = 24576
BANDS = 1024
NX = 256


def draw_neighbours(key, part):
    key = jax.random.fold_in(key, 11)
    reach = ATOM_DEV // 2
    pool_size = 2 * reach - 2
    scores = jax.random.randint(key, (ATOMS, pool_size), 0, 1 << 20) * pool_size + jnp.arange(pool_size, dtype=jnp.int32)[None, :]
    ranked = jnp.argsort(scores, axis=1).astype(jnp.int32)
    chosen = ranked[:, :NB - 3]
    pool_offsets = jnp.where(chosen < reach - 1, chosen - (reach - 1), chosen - (reach - 1) + 1)
    fixed_offsets = jnp.tile(jnp.array([[0, reach, -reach]], dtype=jnp.int32), (ATOMS, 1))
    offsets = jnp.concatenate([fixed_offsets, pool_offsets], axis=1)
    row_ids = jnp.arange(ATOMS, dtype=jnp.int32)[:, None]
    columns = row_ids + offsets
    outside = (columns < 0) | (columns >= ATOMS)
    columns = jnp.where(outside, row_ids - offsets, columns)
    return columns.astype(jnp.int32)


def with_ends(result, rng, least, high):
    index_at = [jax.random.randint(jax.random.fold_in(rng, axis), (), 0, length) for axis, length in enumerate(result.shape)]
    longest = result.shape.index(max(result.shape))
    neighbour = index_at[:longest] + [(index_at[longest] + 1) % result.shape[longest]] + index_at[longest + 1:]
    return result.at[tuple(index_at)].set(least).at[tuple(neighbour)].set(high)


def block_scale(key, shape, cuts, smallest, top_value):
    def one(axis_at, shards_of):
        heights = jax.random.uniform(jax.random.fold_in(jax.random.fold_in(key, 6), axis_at), (shards_of,), jnp.float32, smallest / len(cuts), top_value / len(cuts))
        return jnp.repeat(jnp.exp(heights), shape[axis_at] // shards_of).reshape((-1,) + (1,) * (len(shape) - axis_at - 1))

    level = one(*cuts[0])
    for cut in cuts[1:]:
        level = level * one(*cut)
    return level


def normal_values(key, shape, width, bound, shards=(), held_as=jnp.bfloat16):
    entries = jax.random.normal(key, shape, jnp.float32) * width
    if len(shards) > 0:
        entries = block_scale(key, shape, shards, -0.22, 0.18) * entries
    return jnp.clip(entries, min=-bound, max=bound).astype(held_as)


def setup_inputs(seed: int = 0) -> dict:
    keys = jax.random.split(jax.random.key(seed), 8)
    coefficients = normal_values(keys[0], (2, ORBS, BANDS), 1.0, 6.0, ((1, 32), (2, 8)), jnp.float32)
    hamiltonian = normal_values(keys[1], (ATOMS, NB, ORB, 2 * ORB), (2 * ORB * NB) ** -0.5, 0.15625, ((0, 32),))
    neighbours = draw_neighbours(jax.random.fold_in(keys[7], 71), 0)
    positions = normal_values(keys[3], (3, ATOMS), 0.7, 4.0, (), jnp.float32)
    atom_site = with_ends(jax.random.randint(keys[4], (ATOMS,), 0, GY * GZ), jax.random.fold_in(keys[4], 1), 0, (GY * GZ) - 1).astype(jnp.int32)
    rs_field = normal_values(keys[5], (6, NX, GY, GZ), 1.0, 6.0, ((1, 256),), jnp.float32)
    potential = normal_values(keys[6], (3, NX, GY, GZ), 1.0, 6.0, ((1, 256),), jnp.float32)
    return dict(coefficients=coefficients, hamiltonian=hamiltonian, neighbours=neighbours, positions=positions, atom_site=atom_site, rs_field=rs_field, potential=potential)


coupling = 0.7
elec_step = 1.5
wave_step = 0.5

def derivative(component, dim_index, forward):
    widths = [(0, 0), (0, 0), (0, 0)]
    widths[dim_index] = (0, 1) if forward else (1, 0)
    padded = jnp.pad(component, widths)
    extent = component.shape[dim_index]
    if forward:
        return lax.slice_in_dim(padded, 1, extent + 1, axis=dim_index) - component
    return component - lax.slice_in_dim(padded, 0, extent, axis=dim_index)

def curl_of(part, forward):
    comp_x, comp_y, comp_z = (part[0], part[1], part[2])
    first = derivative(comp_z, 1, forward) - derivative(comp_y, 2, forward)
    second = derivative(comp_x, 2, forward) - derivative(comp_z, 0, forward)
    third = derivative(comp_y, 0, forward) - derivative(comp_x, 1, forward)
    return jnp.stack([first, second, third])

def block_products(ph_real, ph_imag, part_real, part_imag):
    pattern = 'anij,anjk->anik'
    y_real = jnp.einsum(pattern, ph_real, part_real) - jnp.einsum(pattern, ph_imag, part_imag)
    y_imag = jnp.einsum(pattern, ph_real, part_imag) + jnp.einsum(pattern, ph_imag, part_real)
    return (y_real, y_imag)

def reference(coefficients, hamiltonian, neighbours, positions, atom_site, rs_field, potential):
    atom_ids = jnp.arange(ATOMS, dtype=jnp.int32)
    atom_plane = atom_ids * NX // ATOMS
    flat_cell = atom_plane * (GY * GZ) + atom_site
    bond_vectors = positions[:, neighbours] - positions[:, :, None]
    h_real = hamiltonian[..., :ORB].astype(jnp.float32)
    h_imag = hamiltonian[..., ORB:].astype(jnp.float32)
    current_scale = 1.0 / math.sqrt(2.0 * ORB * BANDS)
    coeff = coefficients
    wave_field = rs_field
    vector = potential
    for step_index in range(STEPS):
        at_atoms = vector.reshape(3, -1)[:, flat_cell]
        phase_angle = coupling * lax.optimization_barrier(jnp.sum(0.5 * (at_atoms[:, :, None] + at_atoms[:, neighbours]) * bond_vectors, axis=0))
        cosine = jnp.cos(phase_angle)[:, :, None, None]
        sine_part = jnp.sin(phase_angle)[:, :, None, None]
        ph_real = (h_real * cosine - h_imag * sine_part).astype(jnp.bfloat16).astype(jnp.float32)
        ph_imag = (h_real * sine_part + h_imag * cosine).astype(jnp.bfloat16).astype(jnp.float32)
        taylor_term = coeff.astype(jnp.bfloat16)
        running = coeff
        for order_index in range(1, TERMS + 1):
            own_rows = taylor_term.astype(jnp.float32).reshape(2, ATOMS, ORB, -1)
            blocks = own_rows[:, neighbours]
            y_real, y_imag = block_products(ph_real, ph_imag, blocks[0], blocks[1])
            if order_index == 1:
                block_share = jnp.einsum('aik,anik->an', own_rows[0], y_imag) - jnp.einsum('aik,anik->an', own_rows[1], y_real)
                current = current_scale * lax.optimization_barrier(jnp.sum(bond_vectors * block_share[None], axis=2))
            sum_real = lax.optimization_barrier(jnp.sum(y_real, axis=1))
            sum_imag = lax.optimization_barrier(jnp.sum(y_imag, axis=1))
            factor = elec_step / order_index
            taylor_term = jnp.stack([factor * sum_imag, -factor * sum_real]).reshape(2, ORBS, -1).astype(jnp.bfloat16)
            running = running + taylor_term.astype(jnp.float32)
        coeff = running
        electric = wave_field[0:3]
        magnetic = wave_field[3:6] - wave_step * curl_of(electric, True)
        source = jnp.zeros((3, NX * GY * GZ), jnp.float32).at[:, flat_cell].add(current).reshape(3, NX, GY, GZ)
        electric = electric + wave_step * (curl_of(magnetic, False) - source)
        vector = vector - wave_step * electric
        wave_field = jnp.concatenate([electric, magnetic], axis=0)
    return (coeff, wave_field, vector)
```

```python
import functools
import math

import jax
import jax.numpy as jnp
from jax import lax
from jax.experimental import pallas as pl
from jax.experimental.pallas import tpu as pltpu
from jax.sharding import PartitionSpec as P

TERMS = 3
CHUNKS = 2

coupling = 0.7
elec_step = 1.5
wave_step = 0.5

MESH = pl.DeviceIdType.MESH
F32 = jnp.float32
BF16 = jnp.bfloat16


def iota(shape, dim):
    return lax.broadcasted_iota(jnp.int32, shape, dim)


def shifted(value, dim, forward):
    extent = value.shape[dim]
    moved = pltpu.roll(value, extent - 1 if forward else 1, dim)
    rim = extent - 1 if forward else 0
    return jnp.where(iota(value.shape, dim) == rim, 0.0, moved)


def kernel(
    groups, rows,
    coef_hbm, ham_hbm, nbr, pos, site, field_hbm, pot_hbm,
    coef_out, field_out, pot_out,
    ham, placed, turned, phased, own, vp, halo, weights, inner,
    field, pot, e_send, e_recv, b_send, b_recv,
    at_send, at_recv, cur_send, cur_recv, posb, cos_tab, sin_tab, share,
    in_sem, at_ss, at_rs, cur_ss, cur_rs, t_ss, t_rs, rim_ss, rim_rs,
):
    atoms = nbr.shape[0]
    blocks = nbr.shape[1]
    reach = atoms // 2
    orb = ham.shape[2]
    lanes = 2 * orb
    pairs = atoms // 2
    wide = 2 * reach + 2
    half_rows = reach * orb
    own_rows = atoms * orb
    atoms_all = pos.shape[1]
    planes = groups * rows
    per_row = planes // rows
    sources = 2 * per_row

    g = lax.axis_index("grp")
    r = lax.axis_index("row")
    s = g * rows + r
    q = lax.div(s, per_row)
    m = lax.rem(s, per_row)
    near = m < per_row // 2
    other = jnp.where(near, q - 1, q + 1)
    other_ok = (other >= 0) & (other < rows)

    def owner(p):
        return lax.div(p, rows), lax.rem(p, rows)

    def device(gg, rr):
        return {"grp": gg, "row": rr}

    next_g, next_r = owner(jnp.minimum(s + 1, planes - 1))
    prev_g, prev_r = owner(jnp.maximum(s - 1, 0))
    has_next, has_prev = s < planes - 1, s > 0
    has_up, has_down = r < rows - 1, r > 0

    loads = [
        pltpu.make_async_copy(pot_hbm, pot, in_sem.at[0]),
        pltpu.make_async_copy(coef_hbm, coef_out, in_sem.at[1]),
        pltpu.make_async_copy(ham_hbm, ham, in_sem.at[2]),
        pltpu.make_async_copy(field_hbm, field, in_sem.at[3]),
    ]
    for load in loads:
        load.start()

    barrier = pltpu.get_barrier_semaphore()

    def tell(gg, rr):
        pl.semaphore_signal(barrier, inc=1, device_id=device(gg, rr), device_id_type=MESH)

    first_plane = per_row * r - per_row // 2

    def tell_sources(i, carry):
        p = first_plane + i
        gg, rr = owner(jnp.clip(p, 0, planes - 1))

        @pl.when((p >= 0) & (p < planes) & ((gg != g) | (rr != r)))
        def _():
            tell(gg, rr)

        return carry

    def tell_currents(gg, carry):
        @pl.when((gg != g) | (q != r))
        def _():
            tell(gg, q)

        return carry

    @pl.when(has_next)
    def _():
        tell(next_g, next_r)

    @pl.when(has_prev)
    def _():
        tell(prev_g, prev_r)

    lax.fori_loop(0, sources, tell_sources, 0)
    lax.fori_loop(0, groups, tell_currents, 0)

    first_here = lax.div(3 * s + 1, 2)
    second_ok = lax.rem(s, 2) == 0
    second_here = jnp.minimum(first_here + 1, atoms_all - 1)
    site_one = site[first_here]
    site_two = jnp.where(second_ok, site[second_here], -1)
    grid_y, grid_z = pot.shape[1], pot.shape[2]
    cell = iota((grid_y, grid_z), 0) * grid_z + iota((grid_y, grid_z), 1)
    at_one = cell == site_one
    at_two = cell == site_two
    tile = (8, 128)
    sub8, lane8 = iota(tile, 0), iota(tile, 1)

    loads[0].wait()
    found = []
    for mask in (at_one, at_two):
        for c in range(3):
            hit = jnp.sum(jnp.where(mask, pot[c], 0.0), axis=0, keepdims=True)
            found.append(jnp.sum(hit, axis=1, keepdims=True))
    for k, target in enumerate((q, other)):
        lane_one = first_here - atoms * target + reach
        message = jnp.zeros(tile, F32)
        for j in range(2):
            for c in range(3):
                message = message + jnp.where(
                    (sub8 == c) & (lane8 == lane_one + j), found[3 * j + c], 0.0
                )
        at_send[k] = message

    low_lanes = iota((orb, lanes), 1) < orb
    half = lanes // 2

    def turn(value):
        return pltpu.roll(value, half, 1)

    loads[1].wait()

    def pack(a, carry):
        at = pl.ds(pl.multiple_of(a * orb, orb), orb)
        real = coef_out[0, at, :]
        imag = coef_out[1, at, :]
        real_turned, imag_turned = turn(real), turn(imag)
        first = jnp.where(low_lanes, real, imag_turned)
        first_other = jnp.where(low_lanes, -imag, real_turned)
        second = jnp.where(low_lanes, real_turned, imag)
        second_other = jnp.where(low_lanes, -imag_turned, real)
        for c, (value, rotated) in enumerate(((first, first_other), (second, second_other))):
            value = value.astype(BF16)
            rotated = rotated.astype(BF16)
            own[0, c, at, :] = value
            vp[c, at, :] = rotated
            base = pl.multiple_of((a + reach) * lanes, lanes)
            weights[0, c, pl.ds(base, orb), :] = value
            weights[0, c, pl.ds(base + orb, orb), :] = rotated
        return carry

    lax.fori_loop(0, atoms, pack, 0)

    loads[3].wait()
    for c in range(2):
        e_send[c] = field[1 + c].astype(BF16)

    def ones(cond):
        return jnp.where(cond, 1, 0)

    expected = (
        2 * groups
        + groups * ones(other_ok)
        - 2 * ones(q == r)
        - ones(other_ok & (other == r))
        + ones(has_next)
        + ones(has_prev)
    )
    pl.semaphore_wait(barrier, expected)

    def at_copy(k, slot, gg, rr):
        return pltpu.make_async_remote_copy(
            src_ref=at_send.at[k], dst_ref=at_recv.at[slot],
            send_sem=at_ss.at[k, gg], recv_sem=at_rs.at[slot],
            device_id=device(gg, rr), device_id_type=MESH,
        )

    slot_own = m + per_row // 2
    slot_other = jnp.where(near, m + per_row + per_row // 2, m - per_row // 2)

    def for_at_sends(action, keep):
        for k, (target, slot, ok) in enumerate(
            ((q, slot_own, None), (other, slot_other, other_ok))
        ):
            def one(gg, carry, k=k, target=target, slot=slot, ok=ok):
                is_self = (gg == g) & (target == r)
                go = jnp.logical_not(is_self)
                if ok is not None:
                    go = go & ok

                @pl.when(go)
                def _():
                    action(at_copy(k, slot, gg, target))

                if keep:
                    @pl.when(is_self)
                    def _():
                        at_recv[slot] = at_send[k]

                return carry

            lax.fori_loop(0, groups, one, 0)

    for_at_sends(lambda copy: copy.start(), True)

    def t_copy(k, c, up):
        side = 0 if up else 1
        source = pl.ds(own_rows - half_rows, half_rows) if up else pl.ds(0, half_rows)
        rr = next_r if up else prev_r
        return pltpu.make_async_remote_copy(
            src_ref=own.at[k, c, source, :], dst_ref=halo.at[k, c, side],
            send_sem=t_ss.at[k, c, side], recv_sem=t_rs.at[k, c, side],
            device_id=device(g, rr), device_id_type=MESH,
        )

    def send_term(k, c):
        @pl.when(has_up)
        def _():
            t_copy(k, c, True).start()

        @pl.when(has_down)
        def _():
            t_copy(k, c, False).start()

    for c in range(CHUNKS):
        send_term(0, c)

    e_copy = pltpu.make_async_remote_copy(
        src_ref=e_send, dst_ref=e_recv, send_sem=rim_ss.at[0], recv_sem=rim_rs.at[0],
        device_id=device(prev_g, prev_r), device_id_type=MESH,
    )
    b_copy = pltpu.make_async_remote_copy(
        src_ref=b_send, dst_ref=b_recv, send_sem=rim_ss.at[1], recv_sem=rim_rs.at[1],
        device_id=device(next_g, next_r), device_id_type=MESH,
    )

    @pl.when(has_prev)
    def _():
        e_copy.start()

    loads[2].wait()
    zero_block = jnp.zeros((orb, lanes), F32)
    chunk_rows = 16

    def place(a, carry):
        i = lax.div(a, 2)
        odd = lax.rem(a, 2)
        offsets = [nbr[a, n] - atoms * r - a + reach for n in range(blocks)]

        def piece(part, inner_carry):
            at = pl.multiple_of(part * chunk_rows, chunk_rows)
            to = pl.ds(pl.multiple_of(odd * orb + at, chunk_rows), chunk_rows)
            held = [ham[a, n, pl.ds(at, chunk_rows), :].astype(F32) for n in range(blocks)]
            for d in range(wide - 1):
                who = list(range(3, blocks))
                if d == reach:
                    who = [0] + who
                if d == 0 or d == 2 * reach:
                    who = [1, 2] + who
                total = None
                for n in who:
                    scale = jnp.where(offsets[n] == d, 1.0, 0.0).astype(F32)
                    part_sum = held[n] * scale
                    total = part_sum if total is None else total + part_sum
                lane_at = pl.ds(pl.multiple_of((d + odd) * lanes, lanes), lanes)
                placed[i, to, lane_at] = total
                turned[i, to, lane_at] = turn(total)
            return inner_carry

        lax.fori_loop(0, orb // chunk_rows, piece, 0)
        return carry

    lax.fori_loop(0, atoms, place, 0)
    for i in range(pairs):
        phased[i, 0:orb, (wide - 1) * lanes : wide * lanes] = zero_block.astype(BF16)
        phased[i, orb : 2 * orb, 0:lanes] = zero_block.astype(BF16)

    posb[...] = jnp.zeros(posb.shape, F32)
    posb[0:3, 0:atoms_all] = pos[...]
    shift = lax.rem(2 * posb.shape[1] + reach - atoms * r, posb.shape[1])
    near_pos = pltpu.roll(posb[...], shift, 1)[:, 0:128]
    sub16, lane16 = iota((16, 128), 0), iota((16, 128), 1)

    def column(row, step, offset):
        return jnp.sum(
            jnp.where(lane16 == step * sub16 + offset, row, 0.0), axis=1, keepdims=True
        )

    pos_rows = [near_pos[c : c + 1, :] for c in range(3)]
    pos_cols = [column(row, 1, reach) for row in pos_rows]

    def at_source(i):
        p = first_plane + i
        gg, rr = owner(jnp.clip(p, 0, planes - 1))
        return (p >= 0) & (p < planes), (gg == g) & (rr == r), gg, rr

    def at_wait(i, total):
        ok, is_self, gg, rr = at_source(i)

        @pl.when(ok & jnp.logical_not(is_self))
        def _():
            at_copy(0, i, gg, rr).wait_recv()

        return total

    lax.fori_loop(0, sources, at_wait, 0)
    at_near = jnp.zeros(tile, F32)
    for i in range(sources):
        ok = at_source(i)[0]
        at_near = at_near + jnp.where(ok, at_recv[i], 0.0)

    angle = jnp.zeros((16, 128), F32)
    for c in range(3):
        row = at_near[c : c + 1, :]
        angle = angle + 0.5 * (column(row, 1, reach) + row) * (pos_rows[c] - pos_cols[c])
    angle = coupling * angle
    cosine, sine = jnp.cos(angle), jnp.sin(angle)
    for i in range(pairs):
        back = (128 - 2 * i) % 128
        c_rows, s_rows = cosine, sine
        if back:
            c_rows, s_rows = pltpu.roll(cosine, back, 1), pltpu.roll(sine, back, 1)
        cos_tab[2 * i : 2 * i + 2, :] = c_rows[2 * i : 2 * i + 2, :]
        sin_tab[2 * i : 2 * i + 2, :] = s_rows[2 * i : 2 * i + 2, :]

    signs = jnp.where(iota((1, lanes), 1) < orb, -1.0, 1.0).astype(F32)

    def phase(i, carry):
        for odd in range(2):
            c_row = cos_tab[pl.ds(2 * i + odd, 1), :]
            s_row = sin_tab[pl.ds(2 * i + odd, 1), :]
            at = slice(odd * orb, (odd + 1) * orb)
            for d in range(odd, wide - 1 + odd):
                lane_at = slice(d * lanes, (d + 1) * lanes)
                c_here = jnp.broadcast_to(c_row[:, d : d + 1], (orb, lanes))
                s_here = jnp.broadcast_to(s_row[:, d : d + 1], (1, lanes)) * signs
                phased[i, at, lane_at] = (
                    placed[i, at, lane_at] * c_here + turned[i, at, lane_at] * s_here
                ).astype(BF16)
        return carry

    lax.fori_loop(0, pairs, phase, 0)

    out_signs = -signs
    inner_at, inner_end = reach, reach + atoms

    def dot(left, right):
        return jnp.dot(left, right, preferred_element_type=F32)

    def inner_products(k, c):
        par = k % 2
        for i in range(pairs):
            low, high = max(2 * i, inner_at), min(2 * i + wide, inner_end)
            inner[c, i * lanes : (i + 1) * lanes, :] = dot(
                phased[i, :, (low - 2 * i) * lanes : (high - 2 * i) * lanes],
                weights[par, c, low * lanes : high * lanes, :],
            )

    def take_halo(k, c, up_side):
        par = k % 2
        side = 1 if up_side else 0
        ok = has_up if up_side else has_down

        @pl.when(ok)
        def _():
            t_copy(k, c, not up_side).wait_recv()

        first = inner_end if up_side else 0
        for j in range(reach):
            value = halo[k, c, side, j * orb : (j + 1) * orb, :].astype(F32)
            value = jnp.where(ok, value, 0.0)
            base = (first + j) * lanes
            weights[par, c, base : base + orb, :] = value.astype(BF16)
            weights[par, c, base + orb : base + lanes, :] = (turn(value) * signs).astype(BF16)

    def finish_term(k, c):
        par = k % 2
        factor = elec_step / (k + 1)
        for up_side in (False, True):
            take_halo(k, c, up_side)
            for i in range(pairs // 2):
                if up_side:
                    i = i + pairs // 2
                    low, high = inner_end, 2 * i + wide
                else:
                    low, high = 2 * i, inner_at
                at = slice(i * lanes, (i + 1) * lanes)
                product = factor * (
                    inner[c, at, :]
                    + dot(
                        phased[i, :, (low - 2 * i) * lanes : (high - 2 * i) * lanes],
                        weights[par, c, low * lanes : high * lanes, :],
                    )
                )
                rotated = product.astype(BF16)
                value = (turn(product) * out_signs).astype(BF16)
                own[k + 1, c, at, :] = value
                if k + 1 < TERMS:
                    for j in range(2):
                        base = (inner_at + 2 * i + j) * lanes
                        part = slice(j * orb, (j + 1) * orb)
                        weights[1 - par, c, base : base + orb, :] = value[part]
                        weights[1 - par, c, base + orb : base + lanes, :] = rotated[part]

    def add_terms(which):
        def one(a, carry):
            at = pl.ds(pl.multiple_of(a * orb, orb), orb)
            first = sum(own[k, 0, at, :].astype(F32) for k in which)
            second = sum(own[k, 1, at, :].astype(F32) for k in which)
            coef_out[0, at, :] = coef_out[0, at, :] + jnp.where(low_lanes, first, turn(second))
            coef_out[1, at, :] = coef_out[1, at, :] + jnp.where(low_lanes, turn(first), second)
            return carry

        lax.fori_loop(0, atoms, one, 0)

    for c in range(CHUNKS):
        inner_products(0, c)
    for c in range(CHUNKS):
        finish_term(0, c)
        send_term(1, c)

    @pl.when(has_prev)
    def _():
        e_copy.wait_send()

    @pl.when(has_next)
    def _():
        e_copy.wait_recv()

    comp = [field[c] for c in range(3)]
    ahead = [jnp.where(has_next, e_recv[c].astype(F32), 0.0) for c in range(2)]

    def ahead_y(v):
        return shifted(v, 0, True) - v

    def ahead_z(v):
        return shifted(v, 1, True) - v

    curl = (
        ahead_y(comp[2]) - ahead_z(comp[1]),
        ahead_z(comp[0]) - (ahead[1] - comp[2]),
        (ahead[0] - comp[1]) - ahead_y(comp[0]),
    )
    for c in range(3):
        field_out[3 + c] = field[3 + c] - wave_step * curl[c]
    for c in range(2):
        b_send[c] = field_out[4 + c].astype(BF16)

    @pl.when(has_next)
    def _():
        b_copy.start()

    for c in range(CHUNKS):
        inner_products(1, c)

    def shares(i, carry):
        left = [vp[c, pl.ds(pl.multiple_of(i * lanes, lanes), lanes), :] for c in range(CHUNKS)]
        for d in range(0, wide, 2):
            base = pl.multiple_of(i * 2 * lanes + d * lanes, 2 * lanes)
            rows_at = pl.ds(base, 2 * lanes)
            gram = None
            for c in range(CHUNKS):
                product = lax.dot_general(
                    left[c], weights[0, c, rows_at, :], (((1,), (1,)), ((), ())),
                    preferred_element_type=F32,
                )
                gram = product if gram is None else gram + product
            gram = gram * phased[i, :, d * lanes : (d + 2) * lanes].astype(F32)
            for odd in range(2):
                summed = jnp.sum(gram[odd * orb : (odd + 1) * orb], axis=0, keepdims=True)
                for j in range(2):
                    share[2 * i + odd, d + j : d + j + 1, :] = summed[
                        :, j * lanes : (j + 1) * lanes
                    ]
        return carry

    share[...] = jnp.zeros(share.shape, F32)
    lax.fori_loop(0, pairs, shares, 0)
    scale = 1.0 / math.sqrt(2.0 * orb * groups * lanes)
    for a in range(16):
        if a >= atoms:
            cur_send[a : a + 1, :] = jnp.zeros((1, 128), F32)
            continue
        each = jnp.sum(share[a], axis=1, keepdims=True)
        line = jnp.zeros((1, 128), F32)
        for c in range(3):
            bond = column(pos_rows[c], 1, 2 * (a // 2)) - pos_cols[c][a : a + 1, :]
            value = scale * jnp.sum(each * bond, axis=0, keepdims=True)
            line = line + jnp.where(iota((1, 128), 1) == c, value, 0.0)
        cur_send[a : a + 1, :] = line

    def cur_copy(i, slot, gg, rr):
        return pltpu.make_async_remote_copy(
            src_ref=cur_send, dst_ref=cur_recv.at[slot],
            send_sem=cur_ss.at[i], recv_sem=cur_rs.at[slot],
            device_id=device(gg, rr), device_id_type=MESH,
        )

    def for_cur_sends(action, keep):
        def one(i, carry):
            gg, rr = owner(per_row * r + i)
            is_self = (gg == g) & (rr == r)

            @pl.when(jnp.logical_not(is_self))
            def _():
                action(cur_copy(i, g, gg, rr))

            if keep:
                @pl.when(is_self)
                def _():
                    cur_recv[g] = cur_send[...]

            return carry

        lax.fori_loop(0, per_row, one, 0)

    for_cur_sends(lambda copy: copy.start(), True)

    for c in range(CHUNKS):
        finish_term(1, c)
        send_term(2, c)
    for c in range(CHUNKS):
        inner_products(2, c)
    add_terms((1, 2))

    @pl.when(has_next)
    def _():
        b_copy.wait_send()

    @pl.when(has_prev)
    def _():
        b_copy.wait_recv()

    def cur_wait(gg, carry):
        @pl.when((gg != g) | (q != r))
        def _():
            cur_copy(0, gg, gg, q).wait_recv()

        return carry

    lax.fori_loop(0, groups, cur_wait, 0)
    current = cur_recv[0]
    for gg in range(1, groups):
        current = current + cur_recv[gg]
    atom_one = first_here - atoms * q

    def picked(atom, c):
        hit = jnp.where((sub16 == atom) & (lane16 == c), current, 0.0)
        return jnp.sum(jnp.sum(hit, axis=0, keepdims=True), axis=1, keepdims=True)

    comp = [field_out[3 + c] for c in range(3)]
    behind = [jnp.where(has_prev, b_recv[c].astype(F32), 0.0) for c in range(2)]

    def behind_y(v):
        return v - shifted(v, 0, False)

    def behind_z(v):
        return v - shifted(v, 1, False)

    curl = (
        behind_y(comp[2]) - behind_z(comp[1]),
        behind_z(comp[0]) - (comp[2] - behind[1]),
        (comp[1] - behind[0]) - behind_y(comp[0]),
    )
    for c in range(3):
        source = jnp.where(at_one, picked(atom_one, c), 0.0) + jnp.where(
            at_two, picked(atom_one + 1, c), 0.0
        )
        electric = field[c] + wave_step * (curl[c] - source)
        field_out[c] = electric
        pot_out[c] = pot[c] - wave_step * electric

    for c in range(CHUNKS):
        finish_term(2, c)
    add_terms((3,))

    for_at_sends(lambda copy: copy.wait_send(), False)
    for_cur_sends(lambda copy: copy.wait_send(), False)
    for k in range(TERMS):
        for c in range(CHUNKS):
            @pl.when(has_up)
            def _():
                t_copy(k, c, True).wait_send()

            @pl.when(has_down)
            def _():
                t_copy(k, c, False).wait_send()


def body(groups, rows, coefficients, hamiltonian, neighbours, positions, atom_site, rs_field, potential):
    atoms, blocks, orb = hamiltonian.shape[:3]
    lanes = 2 * orb
    reach = atoms // 2
    pairs = atoms // 2
    wide = 2 * reach + 2
    per_row = groups
    grid = rs_field.shape[2:]
    own_rows = atoms * orb
    field_in = rs_field.reshape((6,) + grid)
    pot_in = potential.reshape((3,) + grid)
    dma = pltpu.SemaphoreType.DMA
    vmem = pl.BlockSpec(memory_space=pltpu.VMEM)
    smem = pl.BlockSpec(memory_space=pltpu.SMEM)
    hbm = pl.BlockSpec(memory_space=pl.ANY)
    coef, field, pot = pl.pallas_call(
        functools.partial(kernel, groups, rows),
        out_shape=(
            jax.ShapeDtypeStruct(coefficients.shape, F32),
            jax.ShapeDtypeStruct(field_in.shape, F32),
            jax.ShapeDtypeStruct(pot_in.shape, F32),
        ),
        in_specs=[hbm, hbm, smem, vmem, smem, hbm, hbm],
        out_specs=(vmem, vmem, vmem),
        scratch_shapes=[
            pltpu.VMEM(hamiltonian.shape, BF16),
            pltpu.VMEM((pairs, 2 * orb, wide * lanes), F32),
            pltpu.VMEM((pairs, 2 * orb, wide * lanes), F32),
            pltpu.VMEM((pairs, 2 * orb, wide * lanes), BF16),
            pltpu.VMEM((TERMS + 1, CHUNKS, own_rows, lanes), BF16),
            pltpu.VMEM((CHUNKS, own_rows, lanes), BF16),
            pltpu.VMEM((TERMS, CHUNKS, 2, reach * orb, lanes), BF16),
            pltpu.VMEM((2, CHUNKS, (atoms + 2 * reach) * lanes, lanes), BF16),
            pltpu.VMEM((CHUNKS, own_rows, lanes), F32),
            pltpu.VMEM(field_in.shape, F32),
            pltpu.VMEM(pot_in.shape, F32),
            pltpu.VMEM((2,) + grid, BF16),
            pltpu.VMEM((2,) + grid, BF16),
            pltpu.VMEM((2,) + grid, BF16),
            pltpu.VMEM((2,) + grid, BF16),
            pltpu.VMEM((2, 8, 128), F32),
            pltpu.VMEM((2 * per_row, 8, 128), F32),
            pltpu.VMEM((16, 128), F32),
            pltpu.VMEM((groups, 16, 128), F32),
            pltpu.VMEM((8, 512), F32),
            pltpu.VMEM((16, 128), F32),
            pltpu.VMEM((16, 128), F32),
            pltpu.VMEM((atoms, 16, 128), F32),
            dma((4,)),
            dma((2, groups)),
            dma((2 * per_row,)),
            dma((per_row,)),
            dma((groups,)),
            dma((TERMS, CHUNKS, 2)),
            dma((TERMS, CHUNKS, 2)),
            dma((2,)),
            dma((2,)),
        ],
        compiler_params=pltpu.CompilerParams(
            collective_id=0, has_side_effects=True, vmem_limit_bytes=48 * 2**20
        ),
    )(coefficients, hamiltonian, neighbours, positions, atom_site, field_in, pot_in)
    return coef, field.reshape(rs_field.shape), pot.reshape(potential.shape)


def solution(mesh):
    placed = (
        P(None, "row", "grp"),
        P("row", None, None, None),
        P("row", None),
        P(),
        P(),
        P(None, ("grp", "row"), None, None),
        P(None, ("grp", "row"), None, None),
    )
    return jax.shard_map(
        functools.partial(body, mesh.shape["grp"], mesh.shape["row"]),
        mesh=mesh,
        in_specs=placed,
        out_specs=(
            P(None, "row", "grp"),
            P(None, ("grp", "row"), None, None),
            P(None, ("grp", "row"), None, None),
        ),
        check_vma=False,
    )
```

```python
import functools
import math

import jax
import jax.numpy as jnp
from jax import lax
from jax.experimental import pallas as pl
from jax.experimental.pallas import tpu as pltpu
from jax.sharding import PartitionSpec as P

TERMS = 3
CHUNKS = 2

coupling = 0.7
elec_step = 1.5
wave_step = 0.5

MESH = pl.DeviceIdType.MESH
F32 = jnp.float32
BF16 = jnp.bfloat16


def iota(shape, dim):
    return lax.broadcasted_iota(jnp.int32, shape, dim)


def shifted(value, dim, forward):
    extent = value.shape[dim]
    moved = pltpu.roll(value, extent - 1 if forward else 1, dim)
    rim = extent - 1 if forward else 0
    return jnp.where(iota(value.shape, dim) == rim, 0.0, moved)


def kernel(
    groups, rows,
    coef_hbm, ham_hbm, nbr_hbm, pos_hbm, site_hbm, field_hbm, pot_hbm,
    coef_res, field_res, pot_res,
    coef_out, field_out, pot_out, nbr, pos, site, ham, placed, turned, phased, own, vp, halo, weights, inner,
    field, pot, e_send, e_recv, b_send, b_recv,
    at_send, at_recv, cur_send, cur_recv, posb, cos_tab, sin_tab, share,
    in_sem, out_sem, at_ss, at_rs, cur_ss, cur_rs, t_ss, t_rs, rim_ss, rim_rs,
):
    atoms = nbr.shape[0]
    blocks = nbr.shape[1]
    reach = atoms // 2
    orb = ham.shape[2]
    lanes = 2 * orb
    pairs = atoms // 2
    wide = 2 * reach + 2
    half_rows = reach * orb
    own_rows = atoms * orb
    atoms_all = pos.shape[1]
    planes = groups * rows
    per_row = planes // rows
    sources = 2 * per_row

    g = lax.axis_index("grp")
    r = lax.axis_index("row")
    s = g * rows + r
    q = lax.div(s, per_row)
    m = lax.rem(s, per_row)
    near = m < per_row // 2
    other = jnp.where(near, q - 1, q + 1)
    other_ok = (other >= 0) & (other < rows)

    def owner(p):
        return lax.div(p, rows), lax.rem(p, rows)

    def device(gg, rr):
        return {"grp": gg, "row": rr}

    next_g, next_r = owner(jnp.minimum(s + 1, planes - 1))
    prev_g, prev_r = owner(jnp.maximum(s - 1, 0))
    has_next, has_prev = s < planes - 1, s > 0
    has_up, has_down = r < rows - 1, r > 0

    loads = [
        pltpu.make_async_copy(source, target, in_sem.at[i])
        for i, (source, target) in enumerate((
            (pot_hbm, pot), (coef_hbm, coef_out), (ham_hbm, ham), (field_hbm, field),
            (site_hbm, site), (nbr_hbm, nbr), (pos_hbm, pos),
        ))
    ]
    for load in loads:
        load.start()

    barrier = pltpu.get_barrier_semaphore()

    def tell(gg, rr):
        pl.semaphore_signal(barrier, inc=1, device_id=device(gg, rr), device_id_type=MESH)

    first_plane = per_row * r - per_row // 2

    def tell_sources(i, carry):
        p = first_plane + i
        gg, rr = owner(jnp.clip(p, 0, planes - 1))

        @pl.when((p >= 0) & (p < planes) & ((gg != g) | (rr != r)))
        def _():
            tell(gg, rr)

        return carry

    def tell_currents(gg, carry):
        @pl.when((gg != g) | (q != r))
        def _():
            tell(gg, q)

        return carry

    @pl.when(has_next)
    def _():
        tell(next_g, next_r)

    @pl.when(has_prev)
    def _():
        tell(prev_g, prev_r)

    lax.fori_loop(0, sources, tell_sources, 0)
    lax.fori_loop(0, groups, tell_currents, 0)

    loads[4].wait()
    first_here = lax.div(3 * s + 1, 2)
    second_ok = lax.rem(s, 2) == 0
    second_here = jnp.minimum(first_here + 1, atoms_all - 1)
    site_one = site[first_here]
    site_two = jnp.where(second_ok, site[second_here], -1)
    grid_y, grid_z = pot.shape[1], pot.shape[2]
    cell = iota((grid_y, grid_z), 0) * grid_z + iota((grid_y, grid_z), 1)
    at_one = cell == site_one
    at_two = cell == site_two
    tile = (1, 128)
    lane1 = iota(tile, 1)
    comp_step = 32

    loads[0].wait()
    found = []
    for mask in (at_one, at_two):
        for c in range(3):
            hit = jnp.sum(jnp.where(mask, pot[c], 0.0), axis=0, keepdims=True)
            found.append(jnp.sum(hit, axis=1, keepdims=True))
    for k, target in enumerate((q, other)):
        lane_one = first_here - atoms * target + reach
        message = jnp.zeros(tile, F32)
        for j in range(2):
            for c in range(3):
                message = message + jnp.where(
                    lane1 == lane_one + j + comp_step * c, found[3 * j + c], 0.0
                )
        at_send[k] = message

    low_lanes = iota((orb, lanes), 1) < orb
    half = lanes // 2

    def turn(value):
        return pltpu.roll(value, half, 1)

    loads[1].wait()

    def pack(a, carry):
        at = pl.ds(pl.multiple_of(a * orb, orb), orb)
        real = coef_out[0, at, :]
        imag = coef_out[1, at, :]
        real_turned, imag_turned = turn(real), turn(imag)
        first = jnp.where(low_lanes, real, imag_turned)
        first_other = jnp.where(low_lanes, -imag, real_turned)
        second = jnp.where(low_lanes, real_turned, imag)
        second_other = jnp.where(low_lanes, -imag_turned, real)
        for c, (value, rotated) in enumerate(((first, first_other), (second, second_other))):
            value = value.astype(BF16)
            rotated = rotated.astype(BF16)
            own[0, c, at, :] = value
            vp[c, at, :] = rotated
            base = pl.multiple_of((a + reach) * lanes, lanes)
            weights[0, c, pl.ds(base, orb), :] = value
            weights[0, c, pl.ds(base + orb, orb), :] = rotated
        return carry

    lax.fori_loop(0, atoms, pack, 0)

    loads[3].wait()
    for c in range(2):
        e_send[c] = field[1 + c].astype(BF16)

    loads[2].wait()
    loads[5].wait()
    zero_block = jnp.zeros((orb, lanes), F32)
    chunk_rows = 16

    def place(a, carry):
        i = lax.div(a, 2)
        odd = lax.rem(a, 2)
        offsets = [nbr[a, n] - atoms * r - a + reach for n in range(blocks)]

        def piece(part, inner_carry):
            at = pl.multiple_of(part * chunk_rows, chunk_rows)
            to = pl.ds(pl.multiple_of(odd * orb + at, chunk_rows), chunk_rows)
            held = [ham[a, n, pl.ds(at, chunk_rows), :].astype(F32) for n in range(blocks)]
            for d in range(wide - 1):
                who = list(range(3, blocks))
                if d == reach:
                    who = [0] + who
                if d == 0 or d == 2 * reach:
                    who = [1, 2] + who
                total = None
                for n in who:
                    scale = jnp.where(offsets[n] == d, 1.0, 0.0).astype(F32)
                    part_sum = held[n] * scale
                    total = part_sum if total is None else total + part_sum
                lane_at = pl.ds(pl.multiple_of((d + odd) * lanes, lanes), lanes)
                placed[i, to, lane_at] = total
                turned[i, to, lane_at] = turn(total)
            return inner_carry

        lax.fori_loop(0, orb // chunk_rows, piece, 0)
        return carry

    lax.fori_loop(0, atoms // 2, place, 0)

    def ones(cond):
        return jnp.where(cond, 1, 0)

    expected = (
        2 * groups
        + groups * ones(other_ok)
        - 2 * ones(q == r)
        - ones(other_ok & (other == r))
        + ones(has_next)
        + ones(has_prev)
    )
    pl.semaphore_wait(barrier, expected)

    def at_copy(k, slot, gg, rr):
        return pltpu.make_async_remote_copy(
            src_ref=at_send.at[k], dst_ref=at_recv.at[slot],
            send_sem=at_ss.at[k, gg], recv_sem=at_rs.at[slot],
            device_id=device(gg, rr), device_id_type=MESH,
        )

    slot_own = m + per_row // 2
    slot_other = jnp.where(near, m + per_row + per_row // 2, m - per_row // 2)

    def for_at_sends(action, keep):
        for k, (target, slot, ok) in enumerate(
            ((q, slot_own, None), (other, slot_other, other_ok))
        ):
            def one(gg, carry, k=k, target=target, slot=slot, ok=ok):
                is_self = (gg == g) & (target == r)
                go = jnp.logical_not(is_self)
                if ok is not None:
                    go = go & ok

                @pl.when(go)
                def _():
                    action(at_copy(k, slot, gg, target))

                if keep:
                    @pl.when(is_self)
                    def _():
                        at_recv[slot] = at_send[k]

                return carry

            lax.fori_loop(0, groups, one, 0)

    for_at_sends(lambda copy: copy.start(), True)

    def t_copy(k, c, up):
        side = 0 if up else 1
        source = pl.ds(own_rows - half_rows, half_rows) if up else pl.ds(0, half_rows)
        rr = next_r if up else prev_r
        return pltpu.make_async_remote_copy(
            src_ref=own.at[k, c, source, :], dst_ref=halo.at[k, c, side],
            send_sem=t_ss.at[k, c, side], recv_sem=t_rs.at[k, c, side],
            device_id=device(g, rr), device_id_type=MESH,
        )

    def send_term(k, c):
        @pl.when(has_up)
        def _():
            t_copy(k, c, True).start()

        @pl.when(has_down)
        def _():
            t_copy(k, c, False).start()

    for c in range(CHUNKS):
        send_term(0, c)

    e_copy = pltpu.make_async_remote_copy(
        src_ref=e_send, dst_ref=e_recv, send_sem=rim_ss.at[0], recv_sem=rim_rs.at[0],
        device_id=device(prev_g, prev_r), device_id_type=MESH,
    )
    b_copy = pltpu.make_async_remote_copy(
        src_ref=b_send, dst_ref=b_recv, send_sem=rim_ss.at[1], recv_sem=rim_rs.at[1],
        device_id=device(next_g, next_r), device_id_type=MESH,
    )

    lax.fori_loop(atoms // 2, atoms, place, 0)
    for i in range(pairs):
        phased[i, 0:orb, (wide - 1) * lanes : wide * lanes] = zero_block.astype(BF16)
        phased[i, orb : 2 * orb, 0:lanes] = zero_block.astype(BF16)

    loads[6].wait()
    posb[...] = jnp.zeros(posb.shape, F32)
    posb[0:3, 0:atoms_all] = pos[...]
    shift = lax.rem(2 * posb.shape[1] + reach - atoms * r, posb.shape[1])
    near_pos = pltpu.roll(posb[...], shift, 1)[:, 0:128]
    sub16, lane16 = iota((16, 128), 0), iota((16, 128), 1)

    def column(row, step, offset):
        return jnp.sum(
            jnp.where(lane16 == step * sub16 + offset, row, 0.0), axis=1, keepdims=True
        )

    pos_rows = [near_pos[c : c + 1, :] for c in range(3)]
    pos_cols = [column(row, 1, reach) for row in pos_rows]

    def at_source(i):
        p = first_plane + i
        gg, rr = owner(jnp.clip(p, 0, planes - 1))
        return (p >= 0) & (p < planes), (gg == g) & (rr == r), gg, rr

    def at_wait(i, total):
        ok, is_self, gg, rr = at_source(i)

        @pl.when(ok & jnp.logical_not(is_self))
        def _():
            at_copy(0, i, gg, rr).wait_recv()

        return total

    lax.fori_loop(0, sources, at_wait, 0)
    at_near = jnp.zeros(tile, F32)
    for i in range(sources):
        ok = at_source(i)[0]
        at_near = at_near + jnp.where(ok, at_recv[i], 0.0)

    angle = jnp.zeros((16, 128), F32)
    for c in range(3):
        row = pltpu.roll(at_near, 128 - comp_step * c, 1) if c else at_near
        angle = angle + 0.5 * (column(row, 1, reach) + row) * (pos_rows[c] - pos_cols[c])
    angle = coupling * angle
    cosine, sine = jnp.cos(angle), jnp.sin(angle)
    for i in range(pairs):
        back = (128 - 2 * i) % 128
        c_rows, s_rows = cosine, sine
        if back:
            c_rows, s_rows = pltpu.roll(cosine, back, 1), pltpu.roll(sine, back, 1)
        cos_tab[2 * i : 2 * i + 2, :] = c_rows[2 * i : 2 * i + 2, :]
        sin_tab[2 * i : 2 * i + 2, :] = s_rows[2 * i : 2 * i + 2, :]

    signs = jnp.where(iota((1, lanes), 1) < orb, -1.0, 1.0).astype(F32)

    def phase(i, carry):
        for odd in range(2):
            c_row = cos_tab[pl.ds(2 * i + odd, 1), :]
            s_row = sin_tab[pl.ds(2 * i + odd, 1), :]
            at = slice(odd * orb, (odd + 1) * orb)
            for d in range(odd, wide - 1 + odd):
                lane_at = slice(d * lanes, (d + 1) * lanes)
                c_here = jnp.broadcast_to(c_row[:, d : d + 1], (orb, lanes))
                s_here = jnp.broadcast_to(s_row[:, d : d + 1], (1, lanes)) * signs
                phased[i, at, lane_at] = (
                    placed[i, at, lane_at] * c_here + turned[i, at, lane_at] * s_here
                ).astype(BF16)
        return carry

    lax.fori_loop(0, pairs, phase, 0)

    out_signs = -signs
    inner_at, inner_end = reach, reach + atoms

    def dot(left, right):
        return jnp.dot(left, right, preferred_element_type=F32)

    def inner_products(k, c):
        par = k % 2
        for i in range(pairs):
            low, high = max(2 * i, inner_at), min(2 * i + wide, inner_end)
            inner[c, i * lanes : (i + 1) * lanes, :] = dot(
                phased[i, :, (low - 2 * i) * lanes : (high - 2 * i) * lanes],
                weights[par, c, low * lanes : high * lanes, :],
            )

    def take_halo(k, c, up_side):
        par = k % 2
        side = 1 if up_side else 0
        ok = has_up if up_side else has_down

        @pl.when(ok)
        def _():
            t_copy(k, c, not up_side).wait_recv()

        first = inner_end if up_side else 0
        for j in range(reach):
            value = halo[k, c, side, j * orb : (j + 1) * orb, :].astype(F32)
            value = jnp.where(ok, value, 0.0)
            base = (first + j) * lanes
            weights[par, c, base : base + orb, :] = value.astype(BF16)
            weights[par, c, base + orb : base + lanes, :] = (turn(value) * signs).astype(BF16)

    def finish_term(k, c):
        par = k % 2
        factor = elec_step / (k + 1)
        for up_side in (False, True):
            take_halo(k, c, up_side)
            for i in range(pairs // 2):
                if up_side:
                    i = i + pairs // 2
                    low, high = inner_end, 2 * i + wide
                else:
                    low, high = 2 * i, inner_at
                at = slice(i * lanes, (i + 1) * lanes)
                product = factor * (
                    inner[c, at, :]
                    + dot(
                        phased[i, :, (low - 2 * i) * lanes : (high - 2 * i) * lanes],
                        weights[par, c, low * lanes : high * lanes, :],
                    )
                )
                rotated = product.astype(BF16)
                value = (turn(product) * out_signs).astype(BF16)
                own[k + 1, c, at, :] = value
                if k + 1 < TERMS:
                    for j in range(2):
                        base = (inner_at + 2 * i + j) * lanes
                        part = slice(j * orb, (j + 1) * orb)
                        weights[1 - par, c, base : base + orb, :] = value[part]
                        weights[1 - par, c, base + orb : base + lanes, :] = rotated[part]

    def add_terms(which):
        def one(a, carry):
            at = pl.ds(pl.multiple_of(a * orb, orb), orb)
            first = sum(own[k, 0, at, :].astype(F32) for k in which)
            second = sum(own[k, 1, at, :].astype(F32) for k in which)
            coef_out[0, at, :] = coef_out[0, at, :] + jnp.where(low_lanes, first, turn(second))
            coef_out[1, at, :] = coef_out[1, at, :] + jnp.where(low_lanes, turn(first), second)
            return carry

        lax.fori_loop(0, atoms, one, 0)

    for c in range(CHUNKS):
        inner_products(0, c)
    for c in range(CHUNKS):
        finish_term(0, c)
        send_term(1, c)

    @pl.when(has_prev)
    def _():
        e_copy.start()

    for c in range(CHUNKS):
        inner_products(1, c)

    def shares(i, carry):
        left = [vp[c, pl.ds(pl.multiple_of(i * lanes, lanes), lanes), :] for c in range(CHUNKS)]
        for d in range(0, wide, 2):
            base = pl.multiple_of(i * 2 * lanes + d * lanes, 2 * lanes)
            rows_at = pl.ds(base, 2 * lanes)
            gram = None
            for c in range(CHUNKS):
                product = lax.dot_general(
                    left[c], weights[0, c, rows_at, :], (((1,), (1,)), ((), ())),
                    preferred_element_type=F32,
                )
                gram = product if gram is None else gram + product
            gram = gram * phased[i, :, d * lanes : (d + 2) * lanes].astype(F32)
            for odd in range(2):
                summed = jnp.sum(gram[odd * orb : (odd + 1) * orb], axis=0, keepdims=True)
                for j in range(2):
                    share[2 * i + odd, d + j : d + j + 1, :] = summed[
                        :, j * lanes : (j + 1) * lanes
                    ]
        return carry

    share[...] = jnp.zeros(share.shape, F32)
    lax.fori_loop(0, pairs, shares, 0)
    scale = 1.0 / math.sqrt(2.0 * orb * groups * lanes)
    line = jnp.zeros(tile, F32)
    for a in range(atoms):
        each = jnp.sum(share[a], axis=1, keepdims=True)
        for c in range(3):
            bond = column(pos_rows[c], 1, 2 * (a // 2)) - pos_cols[c][a : a + 1, :]
            value = scale * jnp.sum(each * bond, axis=0, keepdims=True)
            line = line + jnp.where(lane1 == 4 * a + c, value, 0.0)
    cur_send[...] = line

    def cur_copy(i, slot, gg, rr):
        return pltpu.make_async_remote_copy(
            src_ref=cur_send, dst_ref=cur_recv.at[slot],
            send_sem=cur_ss.at[i], recv_sem=cur_rs.at[slot],
            device_id=device(gg, rr), device_id_type=MESH,
        )

    def for_cur_sends(action, keep):
        def one(i, carry):
            gg, rr = owner(per_row * r + i)
            is_self = (gg == g) & (rr == r)

            @pl.when(jnp.logical_not(is_self))
            def _():
                action(cur_copy(i, g, gg, rr))

            if keep:
                @pl.when(is_self)
                def _():
                    cur_recv[g] = cur_send[...]

            return carry

        lax.fori_loop(0, per_row, one, 0)

    for_cur_sends(lambda copy: copy.start(), True)

    for c in range(CHUNKS):
        finish_term(1, c)
        send_term(2, c)
    @pl.when(has_prev)
    def _():
        e_copy.wait_send()

    @pl.when(has_next)
    def _():
        e_copy.wait_recv()

    comp = [field[c] for c in range(3)]
    ahead = [jnp.where(has_next, e_recv[c].astype(F32), 0.0) for c in range(2)]

    def ahead_y(v):
        return shifted(v, 0, True) - v

    def ahead_z(v):
        return shifted(v, 1, True) - v

    curl = (
        ahead_y(comp[2]) - ahead_z(comp[1]),
        ahead_z(comp[0]) - (ahead[1] - comp[2]),
        (ahead[0] - comp[1]) - ahead_y(comp[0]),
    )
    for c in range(3):
        field_out[3 + c] = field[3 + c] - wave_step * curl[c]
    for c in range(2):
        b_send[c] = field_out[4 + c].astype(BF16)

    @pl.when(has_next)
    def _():
        b_copy.start()

    for c in range(CHUNKS):
        inner_products(2, c)
    add_terms((1, 2))

    @pl.when(has_next)
    def _():
        b_copy.wait_send()

    @pl.when(has_prev)
    def _():
        b_copy.wait_recv()

    def cur_wait(gg, carry):
        @pl.when((gg != g) | (q != r))
        def _():
            cur_copy(0, gg, gg, q).wait_recv()

        return carry

    lax.fori_loop(0, groups, cur_wait, 0)
    current = cur_recv[0]
    for gg in range(1, groups):
        current = current + cur_recv[gg]
    atom_one = first_here - atoms * q

    def picked(atom, c):
        return jnp.sum(jnp.where(lane1 == 4 * atom + c, current, 0.0), axis=1, keepdims=True)

    comp = [field_out[3 + c] for c in range(3)]
    behind = [jnp.where(has_prev, b_recv[c].astype(F32), 0.0) for c in range(2)]

    def behind_y(v):
        return v - shifted(v, 0, False)

    def behind_z(v):
        return v - shifted(v, 1, False)

    curl = (
        behind_y(comp[2]) - behind_z(comp[1]),
        behind_z(comp[0]) - (comp[2] - behind[1]),
        (comp[1] - behind[0]) - behind_y(comp[0]),
    )
    for c in range(3):
        source = jnp.where(at_one, picked(atom_one, c), 0.0) + jnp.where(
            at_two, picked(atom_one + 1, c), 0.0
        )
        electric = field[c] + wave_step * (curl[c] - source)
        field_out[c] = electric
        pot_out[c] = pot[c] - wave_step * electric

    stores = [
        pltpu.make_async_copy(source, target, out_sem.at[i])
        for i, (source, target) in enumerate(
            ((field_out, field_res), (pot_out, pot_res), (coef_out, coef_res))
        )
    ]
    stores[0].start()
    stores[1].start()

    for c in range(CHUNKS):
        finish_term(2, c)
    add_terms((3,))
    stores[2].start()

    for_at_sends(lambda copy: copy.wait_send(), False)
    for_cur_sends(lambda copy: copy.wait_send(), False)
    for k in range(TERMS):
        for c in range(CHUNKS):
            @pl.when(has_up)
            def _():
                t_copy(k, c, True).wait_send()

            @pl.when(has_down)
            def _():
                t_copy(k, c, False).wait_send()
    for store in stores:
        store.wait()


def body(groups, rows, coefficients, hamiltonian, neighbours, positions, atom_site, rs_field, potential):
    atoms, blocks, orb = hamiltonian.shape[:3]
    lanes = 2 * orb
    reach = atoms // 2
    pairs = atoms // 2
    wide = 2 * reach + 2
    per_row = groups
    grid = rs_field.shape[2:]
    own_rows = atoms * orb
    field_in = rs_field.reshape((6,) + grid)
    pot_in = potential.reshape((3,) + grid)
    dma = pltpu.SemaphoreType.DMA
    hbm = pl.BlockSpec(memory_space=pltpu.HBM)
    coef, field, pot = pl.pallas_call(
        functools.partial(kernel, groups, rows),
        out_shape=(
            jax.ShapeDtypeStruct(coefficients.shape, F32),
            jax.ShapeDtypeStruct(field_in.shape, F32),
            jax.ShapeDtypeStruct(pot_in.shape, F32),
        ),
        in_specs=[hbm] * 7,
        out_specs=(hbm, hbm, hbm),
        scratch_shapes=[
            pltpu.VMEM(coefficients.shape, F32),
            pltpu.VMEM(field_in.shape, F32),
            pltpu.VMEM(pot_in.shape, F32),
            pltpu.SMEM(neighbours.shape, jnp.int32),
            pltpu.VMEM(positions.shape, F32),
            pltpu.SMEM(atom_site.shape, jnp.int32),
            pltpu.VMEM(hamiltonian.shape, BF16),
            pltpu.VMEM((pairs, 2 * orb, wide * lanes), F32),
            pltpu.VMEM((pairs, 2 * orb, wide * lanes), F32),
            pltpu.VMEM((pairs, 2 * orb, wide * lanes), BF16),
            pltpu.VMEM((TERMS + 1, CHUNKS, own_rows, lanes), BF16),
            pltpu.VMEM((CHUNKS, own_rows, lanes), BF16),
            pltpu.VMEM((TERMS, CHUNKS, 2, reach * orb, lanes), BF16),
            pltpu.VMEM((2, CHUNKS, (atoms + 2 * reach) * lanes, lanes), BF16),
            pltpu.VMEM((CHUNKS, own_rows, lanes), F32),
            pltpu.VMEM(field_in.shape, F32),
            pltpu.VMEM(pot_in.shape, F32),
            pltpu.VMEM((2,) + grid, BF16),
            pltpu.VMEM((2,) + grid, BF16),
            pltpu.VMEM((2,) + grid, BF16),
            pltpu.VMEM((2,) + grid, BF16),
            pltpu.VMEM((2, 1, 128), F32),
            pltpu.VMEM((2 * per_row, 1, 128), F32),
            pltpu.VMEM((1, 128), F32),
            pltpu.VMEM((groups, 1, 128), F32),
            pltpu.VMEM((8, 512), F32),
            pltpu.VMEM((16, 128), F32),
            pltpu.VMEM((16, 128), F32),
            pltpu.VMEM((atoms, 16, 128), F32),
            dma((7,)),
            dma((3,)),
            dma((2, groups)),
            dma((2 * per_row,)),
            dma((per_row,)),
            dma((groups,)),
            dma((TERMS, CHUNKS, 2)),
            dma((TERMS, CHUNKS, 2)),
            dma((2,)),
            dma((2,)),
        ],
        compiler_params=pltpu.CompilerParams(
            collective_id=0, has_side_effects=True, vmem_limit_bytes=60 * 2**20
        ),
    )(coefficients, hamiltonian, neighbours, positions, atom_site, field_in, pot_in)
    return coef, field.reshape(rs_field.shape), pot.reshape(potential.shape)


def solution(mesh):
    placed = (
        P(None, "row", "grp"),
        P("row", None, None, None),
        P("row", None),
        P(),
        P(),
        P(None, ("grp", "row"), None, None),
        P(None, ("grp", "row"), None, None),
    )
    return jax.shard_map(
        functools.partial(body, mesh.shape["grp"], mesh.shape["row"]),
        mesh=mesh,
        in_specs=placed,
        out_specs=(
            P(None, "row", "grp"),
            P(None, ("grp", "row"), None, None),
            P(None, ("grp", "row"), None, None),
        ),
        check_vma=False,
    )
```

```python
import functools
import math

import jax
import jax.numpy as jnp
from jax import lax
from jax.experimental import pallas as pl
from jax.experimental.pallas import tpu as pltpu
from jax.sharding import PartitionSpec as P

TERMS = 3
CHUNKS = 2

coupling = 0.7
elec_step = 1.5
wave_step = 0.5

MESH = pl.DeviceIdType.MESH
F32 = jnp.float32
BF16 = jnp.bfloat16


def iota(shape, dim):
    return lax.broadcasted_iota(jnp.int32, shape, dim)


def shifted(value, dim, forward):
    extent = value.shape[dim]
    moved = pltpu.roll(value, extent - 1 if forward else 1, dim)
    rim = extent - 1 if forward else 0
    return jnp.where(iota(value.shape, dim) == rim, 0.0, moved)


def kernel(
    groups, rows,
    coef_hbm, ham_hbm, nbr_hbm, pos_hbm, site_hbm, field_hbm, pot_hbm,
    coef_res, field_res, pot_res,
    coef_out, field_out, pot_out, nbr, pos, site, ham, placed, turned, phased, own, vp, halo, weights, inner,
    field, pot, e_send, e_recv, b_send, b_recv,
    at_send, at_recv, cur_send, cur_recv, posb, cos_tab, sin_tab, share,
    in_sem, out_sem, at_ss, at_rs, cur_ss, cur_rs, t_ss, t_rs, rim_ss, rim_rs,
):
    atoms = nbr.shape[0]
    blocks = nbr.shape[1]
    reach = atoms // 2
    orb = ham.shape[2]
    lanes = 2 * orb
    pairs = atoms // 2
    wide = 2 * reach + 2
    half_rows = reach * orb
    own_rows = atoms * orb
    atoms_all = pos.shape[1]
    planes = groups * rows
    per_row = planes // rows
    sources = 2 * per_row

    g = lax.axis_index("grp")
    r = lax.axis_index("row")
    s = g * rows + r
    q = lax.div(s, per_row)
    m = lax.rem(s, per_row)
    near = m < per_row // 2
    other = jnp.where(near, q - 1, q + 1)
    other_ok = (other >= 0) & (other < rows)

    def owner(p):
        return lax.div(p, rows), lax.rem(p, rows)

    def device(gg, rr):
        return {"grp": gg, "row": rr}

    next_g, next_r = owner(jnp.minimum(s + 1, planes - 1))
    prev_g, prev_r = owner(jnp.maximum(s - 1, 0))
    has_next, has_prev = s < planes - 1, s > 0
    has_up, has_down = r < rows - 1, r > 0

    loads = [
        pltpu.make_async_copy(source, target, in_sem.at[i])
        for i, (source, target) in enumerate((
            (pot_hbm, pot), (coef_hbm, coef_out), (ham_hbm, ham), (field_hbm, field),
            (site_hbm, site), (nbr_hbm, nbr), (pos_hbm, pos),
        ))
    ]
    for load in loads:
        load.start()

    barrier = pltpu.get_barrier_semaphore()

    def tell(gg, rr):
        pl.semaphore_signal(barrier, inc=1, device_id=device(gg, rr), device_id_type=MESH)

    first_plane = per_row * r - per_row // 2

    def tell_sources(i, carry):
        p = first_plane + i
        gg, rr = owner(jnp.clip(p, 0, planes - 1))

        @pl.when((p >= 0) & (p < planes) & ((gg != g) | (rr != r)))
        def _():
            tell(gg, rr)

        return carry

    def tell_currents(gg, carry):
        @pl.when((gg != g) | (q != r))
        def _():
            tell(gg, q)

        return carry

    @pl.when(has_next)
    def _():
        tell(next_g, next_r)

    @pl.when(has_prev)
    def _():
        tell(prev_g, prev_r)

    lax.fori_loop(0, sources, tell_sources, 0)
    lax.fori_loop(0, groups, tell_currents, 0)

    loads[4].wait()
    first_here = lax.div(3 * s + 1, 2)
    second_ok = lax.rem(s, 2) == 0
    second_here = jnp.minimum(first_here + 1, atoms_all - 1)
    site_one = site[first_here]
    site_two = jnp.where(second_ok, site[second_here], -1)
    grid_y, grid_z = pot.shape[1], pot.shape[2]
    cell = iota((grid_y, grid_z), 0) * grid_z + iota((grid_y, grid_z), 1)
    at_one = cell == site_one
    at_two = cell == site_two
    tile = (1, 128)
    lane1 = iota(tile, 1)
    comp_step = 32

    loads[0].wait()
    found = []
    for mask in (at_one, at_two):
        for c in range(3):
            hit = jnp.sum(jnp.where(mask, pot[c], 0.0), axis=0, keepdims=True)
            found.append(jnp.sum(hit, axis=1, keepdims=True))
    for k, target in enumerate((q, other)):
        lane_one = first_here - atoms * target + reach
        message = jnp.zeros(tile, F32)
        for j in range(2):
            for c in range(3):
                message = message + jnp.where(
                    lane1 == lane_one + j + comp_step * c, found[3 * j + c], 0.0
                )
        at_send[k] = message

    low_lanes = iota((orb, lanes), 1) < orb
    half = lanes // 2

    def turn(value):
        return pltpu.roll(value, half, 1)

    loads[1].wait()

    def pack(a, carry):
        at = pl.ds(pl.multiple_of(a * orb, orb), orb)
        real = coef_out[0, at, :]
        imag = coef_out[1, at, :]
        real_turned, imag_turned = turn(real), turn(imag)
        first = jnp.where(low_lanes, real, imag_turned)
        first_other = jnp.where(low_lanes, -imag, real_turned)
        second = jnp.where(low_lanes, real_turned, imag)
        second_other = jnp.where(low_lanes, -imag_turned, real)
        for c, (value, rotated) in enumerate(((first, first_other), (second, second_other))):
            value = value.astype(BF16)
            rotated = rotated.astype(BF16)
            own[0, c, at, :] = value
            vp[c, at, :] = rotated
            base = pl.multiple_of((a + reach) * lanes, lanes)
            weights[0, c, pl.ds(base, orb), :] = value
            weights[0, c, pl.ds(base + orb, orb), :] = rotated
        return carry

    lax.fori_loop(0, atoms, pack, 0)

    loads[3].wait()
    for c in range(2):
        e_send[c] = field[1 + c].astype(BF16)

    loads[2].wait()
    loads[5].wait()
    zero_block = jnp.zeros((orb, lanes), F32)
    chunk_rows = 16

    def place(a, carry):
        i = lax.div(a, 2)
        odd = lax.rem(a, 2)
        offsets = [nbr[a, n] - atoms * r - a + reach for n in range(blocks)]

        def piece(part, inner_carry):
            at = pl.multiple_of(part * chunk_rows, chunk_rows)
            to = pl.ds(pl.multiple_of(odd * orb + at, chunk_rows), chunk_rows)
            held = [ham[a, n, pl.ds(at, chunk_rows), :].astype(F32) for n in range(blocks)]
            for d in range(wide - 1):
                who = list(range(3, blocks))
                if d == reach:
                    who = [0] + who
                if d == 0 or d == 2 * reach:
                    who = [1, 2] + who
                total = None
                for n in who:
                    scale = jnp.where(offsets[n] == d, 1.0, 0.0).astype(F32)
                    part_sum = held[n] * scale
                    total = part_sum if total is None else total + part_sum
                lane_at = pl.ds(pl.multiple_of((d + odd) * lanes, lanes), lanes)
                placed[i, to, lane_at] = total
                turned[i, to, lane_at] = turn(total)
            return inner_carry

        lax.fori_loop(0, orb // chunk_rows, piece, 0)
        return carry

    lax.fori_loop(0, atoms // 2, place, 0)

    def ones(cond):
        return jnp.where(cond, 1, 0)

    expected = (
        2 * groups
        + groups * ones(other_ok)
        - 2 * ones(q == r)
        - ones(other_ok & (other == r))
        + ones(has_next)
        + ones(has_prev)
    )
    pl.semaphore_wait(barrier, expected)

    def at_copy(k, slot, gg, rr):
        return pltpu.make_async_remote_copy(
            src_ref=at_send.at[k], dst_ref=at_recv.at[slot],
            send_sem=at_ss.at[k, gg], recv_sem=at_rs.at[slot],
            device_id=device(gg, rr), device_id_type=MESH,
        )

    slot_own = m + per_row // 2
    slot_other = jnp.where(near, m + per_row + per_row // 2, m - per_row // 2)

    def for_at_sends(action, keep):
        for k, (target, slot, ok) in enumerate(
            ((q, slot_own, None), (other, slot_other, other_ok))
        ):
            def one(gg, carry, k=k, target=target, slot=slot, ok=ok):
                is_self = (gg == g) & (target == r)
                go = jnp.logical_not(is_self)
                if ok is not None:
                    go = go & ok

                @pl.when(go)
                def _():
                    action(at_copy(k, slot, gg, target))

                if keep:
                    @pl.when(is_self)
                    def _():
                        at_recv[slot] = at_send[k]

                return carry

            lax.fori_loop(0, groups, one, 0)

    for_at_sends(lambda copy: copy.start(), True)

    def t_copy(k, c, up):
        side = 0 if up else 1
        source = pl.ds(own_rows - half_rows, half_rows) if up else pl.ds(0, half_rows)
        rr = next_r if up else prev_r
        return pltpu.make_async_remote_copy(
            src_ref=own.at[k, c, source, :], dst_ref=halo.at[k, c, side],
            send_sem=t_ss.at[k, c, side], recv_sem=t_rs.at[k, c, side],
            device_id=device(g, rr), device_id_type=MESH,
        )

    def send_term(k, c):
        @pl.when(has_up)
        def _():
            t_copy(k, c, True).start()

        @pl.when(has_down)
        def _():
            t_copy(k, c, False).start()

    send_term(0, 0)

    e_copy = pltpu.make_async_remote_copy(
        src_ref=e_send, dst_ref=e_recv, send_sem=rim_ss.at[0], recv_sem=rim_rs.at[0],
        device_id=device(prev_g, prev_r), device_id_type=MESH,
    )
    b_copy = pltpu.make_async_remote_copy(
        src_ref=b_send, dst_ref=b_recv, send_sem=rim_ss.at[1], recv_sem=rim_rs.at[1],
        device_id=device(next_g, next_r), device_id_type=MESH,
    )

    lax.fori_loop(atoms // 2, atoms, place, 0)
    for c in range(1, CHUNKS):
        send_term(0, c)

    @pl.when(has_prev)
    def _():
        e_copy.start()

    for i in range(pairs):
        phased[i, 0:orb, (wide - 1) * lanes : wide * lanes] = zero_block.astype(BF16)
        phased[i, orb : 2 * orb, 0:lanes] = zero_block.astype(BF16)

    loads[6].wait()
    posb[...] = jnp.zeros(posb.shape, F32)
    posb[0:3, 0:atoms_all] = pos[...]
    shift = lax.rem(2 * posb.shape[1] + reach - atoms * r, posb.shape[1])
    near_pos = pltpu.roll(posb[...], shift, 1)[:, 0:128]
    sub16, lane16 = iota((16, 128), 0), iota((16, 128), 1)

    def column(row, step, offset):
        return jnp.sum(
            jnp.where(lane16 == step * sub16 + offset, row, 0.0), axis=1, keepdims=True
        )

    pos_rows = [near_pos[c : c + 1, :] for c in range(3)]
    pos_cols = [column(row, 1, reach) for row in pos_rows]

    def at_source(i):
        p = first_plane + i
        gg, rr = owner(jnp.clip(p, 0, planes - 1))
        return (p >= 0) & (p < planes), (gg == g) & (rr == r), gg, rr

    def at_wait(i, total):
        ok, is_self, gg, rr = at_source(i)

        @pl.when(ok & jnp.logical_not(is_self))
        def _():
            at_copy(0, i, gg, rr).wait_recv()

        return total

    lax.fori_loop(0, sources, at_wait, 0)
    at_near = jnp.zeros(tile, F32)
    for i in range(sources):
        ok = at_source(i)[0]
        at_near = at_near + jnp.where(ok, at_recv[i], 0.0)

    angle = jnp.zeros((16, 128), F32)
    for c in range(3):
        row = pltpu.roll(at_near, 128 - comp_step * c, 1) if c else at_near
        angle = angle + 0.5 * (column(row, 1, reach) + row) * (pos_rows[c] - pos_cols[c])
    angle = coupling * angle
    cosine, sine = jnp.cos(angle), jnp.sin(angle)
    for i in range(pairs):
        back = (128 - 2 * i) % 128
        c_rows, s_rows = cosine, sine
        if back:
            c_rows, s_rows = pltpu.roll(cosine, back, 1), pltpu.roll(sine, back, 1)
        cos_tab[2 * i : 2 * i + 2, :] = c_rows[2 * i : 2 * i + 2, :]
        sin_tab[2 * i : 2 * i + 2, :] = s_rows[2 * i : 2 * i + 2, :]

    signs = jnp.where(iota((1, lanes), 1) < orb, -1.0, 1.0).astype(F32)

    def phase(i, carry):
        for odd in range(2):
            c_row = cos_tab[pl.ds(2 * i + odd, 1), :]
            s_row = sin_tab[pl.ds(2 * i + odd, 1), :]
            at = slice(odd * orb, (odd + 1) * orb)
            for d in range(odd, wide - 1 + odd):
                lane_at = slice(d * lanes, (d + 1) * lanes)
                c_here = jnp.broadcast_to(c_row[:, d : d + 1], (orb, lanes))
                s_here = jnp.broadcast_to(s_row[:, d : d + 1], (1, lanes)) * signs
                phased[i, at, lane_at] = (
                    placed[i, at, lane_at] * c_here + turned[i, at, lane_at] * s_here
                ).astype(BF16)
        return carry

    lax.fori_loop(0, pairs, phase, 0)

    out_signs = -signs
    inner_at, inner_end = reach, reach + atoms

    def dot(left, right):
        return jnp.dot(left, right, preferred_element_type=F32)

    def inner_products(k, c):
        par = k % 2
        for i in range(pairs):
            low, high = max(2 * i, inner_at), min(2 * i + wide, inner_end)
            inner[c, i * lanes : (i + 1) * lanes, :] = dot(
                phased[i, :, (low - 2 * i) * lanes : (high - 2 * i) * lanes],
                weights[par, c, low * lanes : high * lanes, :],
            )

    def take_halo(k, c, up_side):
        par = k % 2
        side = 1 if up_side else 0
        ok = has_up if up_side else has_down

        @pl.when(ok)
        def _():
            t_copy(k, c, not up_side).wait_recv()

        first = inner_end if up_side else 0
        for j in range(reach):
            value = halo[k, c, side, j * orb : (j + 1) * orb, :].astype(F32)
            value = jnp.where(ok, value, 0.0)
            base = (first + j) * lanes
            weights[par, c, base : base + orb, :] = value.astype(BF16)
            weights[par, c, base + orb : base + lanes, :] = (turn(value) * signs).astype(BF16)

    def finish_term(k, c):
        par = k % 2
        factor = elec_step / (k + 1)
        for up_side in (False, True):
            take_halo(k, c, up_side)
            for i in range(pairs // 2):
                if up_side:
                    i = i + pairs // 2
                    low, high = inner_end, 2 * i + wide
                else:
                    low, high = 2 * i, inner_at
                at = slice(i * lanes, (i + 1) * lanes)
                product = factor * (
                    inner[c, at, :]
                    + dot(
                        phased[i, :, (low - 2 * i) * lanes : (high - 2 * i) * lanes],
                        weights[par, c, low * lanes : high * lanes, :],
                    )
                )
                rotated = product.astype(BF16)
                value = (turn(product) * out_signs).astype(BF16)
                if k + 1 == TERMS and c + 1 == CHUNKS:
                    first = own[k + 1, 0, at, :].astype(F32)
                    second = value.astype(F32)
                    low = iota((1, lanes), 1) < orb
                    coef_out[0, at, :] = coef_out[0, at, :] + jnp.where(low, first, turn(second))
                    coef_out[1, at, :] = coef_out[1, at, :] + jnp.where(low, turn(first), second)
                    continue
                own[k + 1, c, at, :] = value
                if k + 1 < TERMS:
                    for j in range(2):
                        base = (inner_at + 2 * i + j) * lanes
                        part = slice(j * orb, (j + 1) * orb)
                        weights[1 - par, c, base : base + orb, :] = value[part]
                        weights[1 - par, c, base + orb : base + lanes, :] = rotated[part]

    def add_terms(which):
        def one(a, carry):
            at = pl.ds(pl.multiple_of(a * orb, orb), orb)
            first = sum(own[k, 0, at, :].astype(F32) for k in which)
            second = sum(own[k, 1, at, :].astype(F32) for k in which)
            coef_out[0, at, :] = coef_out[0, at, :] + jnp.where(low_lanes, first, turn(second))
            coef_out[1, at, :] = coef_out[1, at, :] + jnp.where(low_lanes, turn(first), second)
            return carry

        lax.fori_loop(0, atoms, one, 0)

    for c in range(CHUNKS):
        inner_products(0, c)
    for c in range(CHUNKS):
        finish_term(0, c)
        send_term(1, c)
        inner_products(1, c)

    def shares(i, carry):
        left = [vp[c, pl.ds(pl.multiple_of(i * lanes, lanes), lanes), :] for c in range(CHUNKS)]
        for d in range(0, wide, 2):
            base = pl.multiple_of(i * 2 * lanes + d * lanes, 2 * lanes)
            rows_at = pl.ds(base, 2 * lanes)
            gram = None
            for c in range(CHUNKS):
                product = lax.dot_general(
                    left[c], weights[0, c, rows_at, :], (((1,), (1,)), ((), ())),
                    preferred_element_type=F32,
                )
                gram = product if gram is None else gram + product
            gram = gram * phased[i, :, d * lanes : (d + 2) * lanes].astype(F32)
            for odd in range(2):
                summed = jnp.sum(gram[odd * orb : (odd + 1) * orb], axis=0, keepdims=True)
                for j in range(2):
                    share[2 * i + odd, d + j : d + j + 1, :] = summed[
                        :, j * lanes : (j + 1) * lanes
                    ]
        return carry

    share[...] = jnp.zeros(share.shape, F32)
    lax.fori_loop(0, pairs, shares, 0)
    scale = 1.0 / math.sqrt(2.0 * orb * groups * lanes)
    line = jnp.zeros(tile, F32)
    for a in range(atoms):
        each = jnp.sum(share[a], axis=1, keepdims=True)
        for c in range(3):
            bond = column(pos_rows[c], 1, 2 * (a // 2)) - pos_cols[c][a : a + 1, :]
            value = scale * jnp.sum(each * bond, axis=0, keepdims=True)
            line = line + jnp.where(lane1 == 4 * a + c, value, 0.0)
    cur_send[...] = line

    def cur_copy(i, slot, gg, rr):
        return pltpu.make_async_remote_copy(
            src_ref=cur_send, dst_ref=cur_recv.at[slot],
            send_sem=cur_ss.at[i], recv_sem=cur_rs.at[slot],
            device_id=device(gg, rr), device_id_type=MESH,
        )

    def for_cur_sends(action, keep):
        def one(i, carry):
            gg, rr = owner(per_row * r + i)
            is_self = (gg == g) & (rr == r)

            @pl.when(jnp.logical_not(is_self))
            def _():
                action(cur_copy(i, g, gg, rr))

            if keep:
                @pl.when(is_self)
                def _():
                    cur_recv[g] = cur_send[...]

            return carry

        lax.fori_loop(0, per_row, one, 0)

    for_cur_sends(lambda copy: copy.start(), True)

    @pl.when(has_prev)
    def _():
        e_copy.wait_send()

    @pl.when(has_next)
    def _():
        e_copy.wait_recv()

    comp = [field[c] for c in range(3)]
    ahead = [jnp.where(has_next, e_recv[c].astype(F32), 0.0) for c in range(2)]

    def ahead_y(v):
        return shifted(v, 0, True) - v

    def ahead_z(v):
        return shifted(v, 1, True) - v

    curl = (
        ahead_y(comp[2]) - ahead_z(comp[1]),
        ahead_z(comp[0]) - (ahead[1] - comp[2]),
        (ahead[0] - comp[1]) - ahead_y(comp[0]),
    )
    for c in range(3):
        field_out[3 + c] = field[3 + c] - wave_step * curl[c]
    for c in range(2):
        b_send[c] = field_out[4 + c].astype(BF16)

    @pl.when(has_next)
    def _():
        b_copy.start()

    for c in range(CHUNKS):
        finish_term(1, c)
        send_term(2, c)
        inner_products(2, c)
    add_terms((1, 2))

    @pl.when(has_next)
    def _():
        b_copy.wait_send()

    @pl.when(has_prev)
    def _():
        b_copy.wait_recv()

    def cur_wait(gg, carry):
        @pl.when((gg != g) | (q != r))
        def _():
            cur_copy(0, gg, gg, q).wait_recv()

        return carry

    lax.fori_loop(0, groups, cur_wait, 0)
    current = cur_recv[0]
    for gg in range(1, groups):
        current = current + cur_recv[gg]
    atom_one = first_here - atoms * q

    def picked(atom, c):
        return jnp.sum(jnp.where(lane1 == 4 * atom + c, current, 0.0), axis=1, keepdims=True)

    comp = [field_out[3 + c] for c in range(3)]
    behind = [jnp.where(has_prev, b_recv[c].astype(F32), 0.0) for c in range(2)]

    def behind_y(v):
        return v - shifted(v, 0, False)

    def behind_z(v):
        return v - shifted(v, 1, False)

    curl = (
        behind_y(comp[2]) - behind_z(comp[1]),
        behind_z(comp[0]) - (comp[2] - behind[1]),
        (comp[1] - behind[0]) - behind_y(comp[0]),
    )
    for c in range(3):
        source = jnp.where(at_one, picked(atom_one, c), 0.0) + jnp.where(
            at_two, picked(atom_one + 1, c), 0.0
        )
        electric = field[c] + wave_step * (curl[c] - source)
        field_out[c] = electric
        pot_out[c] = pot[c] - wave_step * electric

    stores = [
        pltpu.make_async_copy(source, target, out_sem.at[i])
        for i, (source, target) in enumerate(
            ((field_out, field_res), (pot_out, pot_res), (coef_out, coef_res))
        )
    ]
    stores[0].start()
    stores[1].start()

    for c in range(CHUNKS):
        finish_term(2, c)
    stores[2].start()

    for_at_sends(lambda copy: copy.wait_send(), False)
    for_cur_sends(lambda copy: copy.wait_send(), False)
    for k in range(TERMS):
        for c in range(CHUNKS):
            @pl.when(has_up)
            def _():
                t_copy(k, c, True).wait_send()

            @pl.when(has_down)
            def _():
                t_copy(k, c, False).wait_send()
    for store in stores:
        store.wait()


def hand_on(coef, field, pot, coef_out, field_out, pot_out, coef_buf, field_buf, pot_buf, in_sem, out_sem):
    half = coef.shape[1] // 2
    pieces = [(pot, pot_buf, pot_out)]
    for i in range(2):
        pieces.append([ref.at[pl.ds(3 * i, 3)] for ref in (field, field_buf, field_out)])
        for part in range(2):
            at = pl.ds(part * half, half)
            pieces.append([ref.at[i, at] for ref in (coef, coef_buf, coef_out)])
    loads, stores = [], []
    for i, piece in enumerate(pieces):
        source, held, target = piece
        loads.append(pltpu.make_async_copy(source, held, in_sem.at[i]))
        stores.append(pltpu.make_async_copy(held, target, out_sem.at[i]))
    for load in loads:
        load.start()
    for load, store in zip(loads, stores):
        load.wait()
        store.start()
    for store in stores:
        store.wait()


def body(groups, rows, coefficients, hamiltonian, neighbours, positions, atom_site, rs_field, potential):
    atoms, blocks, orb = hamiltonian.shape[:3]
    lanes = 2 * orb
    reach = atoms // 2
    pairs = atoms // 2
    wide = 2 * reach + 2
    per_row = groups
    grid = rs_field.shape[2:]
    own_rows = atoms * orb
    field_in = rs_field.reshape((6,) + grid)
    pot_in = potential.reshape((3,) + grid)
    dma = pltpu.SemaphoreType.DMA
    hbm = pl.BlockSpec(memory_space=pltpu.HBM)
    coef, field, pot = pl.pallas_call(
        functools.partial(kernel, groups, rows),
        out_shape=(
            jax.ShapeDtypeStruct(coefficients.shape, F32),
            jax.ShapeDtypeStruct(field_in.shape, F32),
            jax.ShapeDtypeStruct(pot_in.shape, F32),
        ),
        in_specs=[hbm] * 7,
        out_specs=(hbm, hbm, hbm),
        scratch_shapes=[
            pltpu.VMEM(coefficients.shape, F32),
            pltpu.VMEM(field_in.shape, F32),
            pltpu.VMEM(pot_in.shape, F32),
            pltpu.SMEM(neighbours.shape, jnp.int32),
            pltpu.VMEM(positions.shape, F32),
            pltpu.SMEM(atom_site.shape, jnp.int32),
            pltpu.VMEM(hamiltonian.shape, BF16),
            pltpu.VMEM((pairs, 2 * orb, wide * lanes), F32),
            pltpu.VMEM((pairs, 2 * orb, wide * lanes), F32),
            pltpu.VMEM((pairs, 2 * orb, wide * lanes), BF16),
            pltpu.VMEM((TERMS + 1, CHUNKS, own_rows, lanes), BF16),
            pltpu.VMEM((CHUNKS, own_rows, lanes), BF16),
            pltpu.VMEM((TERMS, CHUNKS, 2, reach * orb, lanes), BF16),
            pltpu.VMEM((2, CHUNKS, (atoms + 2 * reach) * lanes, lanes), BF16),
            pltpu.VMEM((CHUNKS, own_rows, lanes), F32),
            pltpu.VMEM(field_in.shape, F32),
            pltpu.VMEM(pot_in.shape, F32),
            pltpu.VMEM((2,) + grid, BF16),
            pltpu.VMEM((2,) + grid, BF16),
            pltpu.VMEM((2,) + grid, BF16),
            pltpu.VMEM((2,) + grid, BF16),
            pltpu.VMEM((2, 1, 128), F32),
            pltpu.VMEM((2 * per_row, 1, 128), F32),
            pltpu.VMEM((1, 128), F32),
            pltpu.VMEM((groups, 1, 128), F32),
            pltpu.VMEM((8, 512), F32),
            pltpu.VMEM((16, 128), F32),
            pltpu.VMEM((16, 128), F32),
            pltpu.VMEM((atoms, 16, 128), F32),
            dma((7,)),
            dma((3,)),
            dma((2, groups)),
            dma((2 * per_row,)),
            dma((per_row,)),
            dma((groups,)),
            dma((TERMS, CHUNKS, 2)),
            dma((TERMS, CHUNKS, 2)),
            dma((2,)),
            dma((2,)),
        ],
        compiler_params=pltpu.CompilerParams(
            collective_id=0, has_side_effects=True, vmem_limit_bytes=60 * 2**20
        ),
    )(coefficients, hamiltonian, neighbours, positions, atom_site, field_in, pot_in)
    coef, field, pot = pl.pallas_call(
        hand_on,
        out_shape=(
            jax.ShapeDtypeStruct(coefficients.shape, F32),
            jax.ShapeDtypeStruct(field_in.shape, F32),
            jax.ShapeDtypeStruct(pot_in.shape, F32),
        ),
        in_specs=[hbm, hbm, hbm],
        out_specs=(hbm, hbm, hbm),
        scratch_shapes=[
            pltpu.VMEM(coefficients.shape, F32),
            pltpu.VMEM(field_in.shape, F32),
            pltpu.VMEM(pot_in.shape, F32),
            dma((8,)),
            dma((8,)),
        ],
        compiler_params=pltpu.CompilerParams(vmem_limit_bytes=60 * 2**20),
    )(coef, field, pot)
    return coef, field.reshape(rs_field.shape), pot.reshape(potential.shape)


def solution(mesh):
    placed = (
        P(None, "row", "grp"),
        P("row", None, None, None),
        P("row", None),
        P(),
        P(),
        P(None, ("grp", "row"), None, None),
        P(None, ("grp", "row"), None, None),
    )
    return jax.shard_map(
        functools.partial(body, mesh.shape["grp"], mesh.shape["row"]),
        mesh=mesh,
        in_specs=placed,
        out_specs=(
            P(None, "row", "grp"),
            P(None, ("grp", "row"), None, None),
            P(None, ("grp", "row"), None, None),
        ),
        check_vma=False,
    )
```

```python
import functools
import math

import jax
import jax.numpy as jnp
from jax import lax
from jax.experimental import pallas as pl
from jax.experimental.pallas import tpu as pltpu
from jax.sharding import PartitionSpec as P

TERMS = 3
CHUNKS = 2

coupling = 0.7
elec_step = 1.5
wave_step = 0.5

MESH = pl.DeviceIdType.MESH
F32 = jnp.float32
BF16 = jnp.bfloat16


def iota(shape, dim):
    return lax.broadcasted_iota(jnp.int32, shape, dim)


def shifted(value, dim, forward):
    extent = value.shape[dim]
    moved = pltpu.roll(value, extent - 1 if forward else 1, dim)
    rim = extent - 1 if forward else 0
    return jnp.where(iota(value.shape, dim) == rim, 0.0, moved)


def kernel(
    groups, rows,
    coef_hbm, ham_hbm, nbr_hbm, pos_hbm, site_hbm, field_hbm, pot_hbm,
    coef_res, field_res, pot_res,
    coef_out, field_out, pot_out, nbr, pos, site, ham, placed, turned, phased, own, vp, halo, weights, inner,
    field, pot, e_send, e_recv, b_send, b_recv,
    at_send, at_recv, cur_send, cur_recv, posb, cos_tab, sin_tab, share,
    in_sem, out_sem, at_ss, at_rs, cur_ss, cur_rs, t_ss, t_rs, rim_ss, rim_rs,
):
    atoms = nbr.shape[0]
    blocks = nbr.shape[1]
    reach = atoms // 2
    orb = ham.shape[2]
    lanes = 2 * orb
    pairs = atoms // 2
    wide = 2 * reach + 2
    half_rows = reach * orb
    own_rows = atoms * orb
    atoms_all = pos.shape[1]
    planes = groups * rows
    per_row = planes // rows
    sources = 2 * per_row

    g = lax.axis_index("grp")
    r = lax.axis_index("row")
    s = g * rows + r
    q = lax.div(s, per_row)
    m = lax.rem(s, per_row)
    near = m < per_row // 2
    other = jnp.where(near, q - 1, q + 1)
    other_ok = (other >= 0) & (other < rows)

    def owner(p):
        return lax.div(p, rows), lax.rem(p, rows)

    def device(gg, rr):
        return {"grp": gg, "row": rr}

    next_g, next_r = owner(jnp.minimum(s + 1, planes - 1))
    prev_g, prev_r = owner(jnp.maximum(s - 1, 0))
    has_next, has_prev = s < planes - 1, s > 0
    has_up, has_down = r < rows - 1, r > 0

    loads = [
        pltpu.make_async_copy(source, target, in_sem.at[i])
        for i, (source, target) in enumerate((
            (pot_hbm, pot), (coef_hbm, coef_out), (ham_hbm, ham), (field_hbm, field),
            (site_hbm, site), (nbr_hbm, nbr), (pos_hbm, pos),
        ))
    ]
    for load in loads:
        load.start()

    barrier = pltpu.get_barrier_semaphore()

    def tell(gg, rr):
        pl.semaphore_signal(barrier, inc=1, device_id=device(gg, rr), device_id_type=MESH)

    first_plane = per_row * r - per_row // 2

    def tell_sources(i, carry):
        p = first_plane + i
        gg, rr = owner(jnp.clip(p, 0, planes - 1))

        @pl.when((p >= 0) & (p < planes) & ((gg != g) | (rr != r)))
        def _():
            tell(gg, rr)

        return carry

    def tell_currents(gg, carry):
        @pl.when((gg != g) | (q != r))
        def _():
            tell(gg, q)

        return carry

    @pl.when(has_next)
    def _():
        tell(next_g, next_r)

    @pl.when(has_prev)
    def _():
        tell(prev_g, prev_r)

    lax.fori_loop(0, sources, tell_sources, 0)

    loads[4].wait()
    first_here = lax.div(3 * s + 1, 2)
    second_ok = lax.rem(s, 2) == 0
    second_here = jnp.minimum(first_here + 1, atoms_all - 1)
    site_one = site[first_here]
    site_two = jnp.where(second_ok, site[second_here], -1)
    grid_y, grid_z = pot.shape[1], pot.shape[2]
    cell = iota((grid_y, grid_z), 0) * grid_z + iota((grid_y, grid_z), 1)
    at_one = cell == site_one
    at_two = cell == site_two
    tile = (1, 128)
    lane1 = iota(tile, 1)
    comp_step = 32

    loads[0].wait()
    found = []
    for mask in (at_one, at_two):
        for c in range(3):
            hit = jnp.sum(jnp.where(mask, pot[c], 0.0), axis=0, keepdims=True)
            found.append(jnp.sum(hit, axis=1, keepdims=True))
    for k, target in enumerate((q, other)):
        lane_one = first_here - atoms * target + reach
        message = jnp.zeros(tile, F32)
        for j in range(2):
            for c in range(3):
                message = message + jnp.where(
                    lane1 == lane_one + j + comp_step * c, found[3 * j + c], 0.0
                )
        at_send[k] = message

    low_lanes = iota((orb, lanes), 1) < orb
    half = lanes // 2

    def turn(value):
        return pltpu.roll(value, half, 1)

    loads[1].wait()

    def pack(a, carry):
        at = pl.ds(pl.multiple_of(a * orb, orb), orb)
        real = coef_out[0, at, :]
        imag = coef_out[1, at, :]
        real_turned, imag_turned = turn(real), turn(imag)
        first = jnp.where(low_lanes, real, imag_turned)
        first_other = jnp.where(low_lanes, -imag, real_turned)
        second = jnp.where(low_lanes, real_turned, imag)
        second_other = jnp.where(low_lanes, -imag_turned, real)
        for c, (value, rotated) in enumerate(((first, first_other), (second, second_other))):
            value = value.astype(BF16)
            rotated = rotated.astype(BF16)
            own[0, c, at, :] = value
            vp[c, at, :] = rotated
            base = pl.multiple_of((a + reach) * lanes, lanes)
            weights[0, c, pl.ds(base, orb), :] = value
            weights[0, c, pl.ds(base + orb, orb), :] = rotated
        return carry

    lax.fori_loop(0, atoms, pack, 0)

    loads[3].wait()
    for c in range(2):
        e_send[c] = field[1 + c].astype(BF16)

    loads[2].wait()
    loads[5].wait()
    zero_block = jnp.zeros((orb, lanes), F32)
    chunk_rows = 32

    def place(a, carry):
        i = lax.div(a, 2)
        odd = lax.rem(a, 2)
        offsets = [nbr[a, n] - atoms * r - a + reach for n in range(blocks)]

        def piece(part, inner_carry):
            at = pl.multiple_of(part * chunk_rows, chunk_rows)
            to = pl.ds(pl.multiple_of(odd * orb + at, chunk_rows), chunk_rows)
            held = [ham[a, n, pl.ds(at, chunk_rows), :].astype(F32) for n in range(blocks)]
            for d in range(wide - 1):
                who = list(range(3, blocks))
                if d == reach:
                    who = [0] + who
                if d == 0 or d == 2 * reach:
                    who = [1, 2] + who
                total = None
                for n in who:
                    scale = jnp.where(offsets[n] == d, 1.0, 0.0).astype(F32)
                    part_sum = held[n] * scale
                    total = part_sum if total is None else total + part_sum
                lane_at = pl.ds(pl.multiple_of((d + odd) * lanes, lanes), lanes)
                placed[i, to, lane_at] = total
                turned[i, to, lane_at] = turn(total)
            return inner_carry

        lax.fori_loop(0, orb // chunk_rows, piece, 0)
        return carry

    def ones(cond):
        return jnp.where(cond, 1, 0)

    expected = (
        groups
        + groups * ones(other_ok)
        - ones(q == r)
        - ones(other_ok & (other == r))
        + ones(has_next)
        + ones(has_prev)
    )
    pl.semaphore_wait(barrier, expected)

    def at_copy(k, slot, gg, rr):
        return pltpu.make_async_remote_copy(
            src_ref=at_send.at[k], dst_ref=at_recv.at[slot],
            send_sem=at_ss.at[k, gg], recv_sem=at_rs.at[slot],
            device_id=device(gg, rr), device_id_type=MESH,
        )

    slot_own = m + per_row // 2
    slot_other = jnp.where(near, m + per_row + per_row // 2, m - per_row // 2)

    def for_at_sends(action, keep):
        for k, (target, slot, ok) in enumerate(
            ((q, slot_own, None), (other, slot_other, other_ok))
        ):
            def one(gg, carry, k=k, target=target, slot=slot, ok=ok):
                is_self = (gg == g) & (target == r)
                go = jnp.logical_not(is_self)
                if ok is not None:
                    go = go & ok

                @pl.when(go)
                def _():
                    action(at_copy(k, slot, gg, target))

                if keep:
                    @pl.when(is_self)
                    def _():
                        at_recv[slot] = at_send[k]

                return carry

            lax.fori_loop(0, groups, one, 0)

    for_at_sends(lambda copy: copy.start(), True)

    def t_copy(k, c, up):
        side = 0 if up else 1
        source = pl.ds(own_rows - half_rows, half_rows) if up else pl.ds(0, half_rows)
        rr = next_r if up else prev_r
        return pltpu.make_async_remote_copy(
            src_ref=own.at[k, c, source, :], dst_ref=halo.at[k, c, side],
            send_sem=t_ss.at[k, c, side], recv_sem=t_rs.at[k, c, side],
            device_id=device(g, rr), device_id_type=MESH,
        )

    def send_term(k, c):
        @pl.when(has_up)
        def _():
            t_copy(k, c, True).start()

        @pl.when(has_down)
        def _():
            t_copy(k, c, False).start()

    send_term(0, 0)

    e_copy = pltpu.make_async_remote_copy(
        src_ref=e_send, dst_ref=e_recv, send_sem=rim_ss.at[0], recv_sem=rim_rs.at[0],
        device_id=device(prev_g, prev_r), device_id_type=MESH,
    )
    b_copy = pltpu.make_async_remote_copy(
        src_ref=b_send, dst_ref=b_recv, send_sem=rim_ss.at[1], recv_sem=rim_rs.at[1],
        device_id=device(next_g, next_r), device_id_type=MESH,
    )

    lax.fori_loop(0, 6, place, 0)
    for c in range(1, CHUNKS):
        send_term(0, c)

    lax.fori_loop(6, atoms, place, 0)
    @pl.when(has_prev)
    def _():
        e_copy.start()

    for i in range(pairs):
        phased[i, 0:orb, (wide - 1) * lanes : wide * lanes] = zero_block.astype(BF16)
        phased[i, orb : 2 * orb, 0:lanes] = zero_block.astype(BF16)

    loads[6].wait()
    posb[...] = jnp.zeros(posb.shape, F32)
    posb[0:3, 0:atoms_all] = pos[...]
    shift = lax.rem(2 * posb.shape[1] + reach - atoms * r, posb.shape[1])
    near_pos = pltpu.roll(posb[...], shift, 1)[:, 0:128]
    sub16, lane16 = iota((16, 128), 0), iota((16, 128), 1)

    def column(row, step, offset):
        return jnp.sum(
            jnp.where(lane16 == step * sub16 + offset, row, 0.0), axis=1, keepdims=True
        )

    pos_rows = [near_pos[c : c + 1, :] for c in range(3)]
    pos_cols = [column(row, 1, reach) for row in pos_rows]

    def at_source(i):
        p = first_plane + i
        gg, rr = owner(jnp.clip(p, 0, planes - 1))
        return (p >= 0) & (p < planes), (gg == g) & (rr == r), gg, rr

    def at_wait(i, total):
        ok, is_self, gg, rr = at_source(i)

        @pl.when(ok & jnp.logical_not(is_self))
        def _():
            at_copy(0, i, gg, rr).wait_recv()

        return total

    lax.fori_loop(0, sources, at_wait, 0)
    at_near = jnp.zeros(tile, F32)
    for i in range(sources):
        ok = at_source(i)[0]
        at_near = at_near + jnp.where(ok, at_recv[i], 0.0)

    angle = jnp.zeros((16, 128), F32)
    for c in range(3):
        row = pltpu.roll(at_near, 128 - comp_step * c, 1) if c else at_near
        angle = angle + 0.5 * (column(row, 1, reach) + row) * (pos_rows[c] - pos_cols[c])
    angle = coupling * angle
    cosine, sine = jnp.cos(angle), jnp.sin(angle)
    for i in range(pairs):
        back = (128 - 2 * i) % 128
        c_rows, s_rows = cosine, sine
        if back:
            c_rows, s_rows = pltpu.roll(cosine, back, 1), pltpu.roll(sine, back, 1)
        cos_tab[2 * i : 2 * i + 2, :] = c_rows[2 * i : 2 * i + 2, :]
        sin_tab[2 * i : 2 * i + 2, :] = s_rows[2 * i : 2 * i + 2, :]

    signs = jnp.where(iota((1, lanes), 1) < orb, -1.0, 1.0).astype(F32)

    def phase(i, carry):
        for odd in range(2):
            c_row = cos_tab[pl.ds(2 * i + odd, 1), :]
            s_row = sin_tab[pl.ds(2 * i + odd, 1), :]
            at = slice(odd * orb, (odd + 1) * orb)
            for d in range(odd, wide - 1 + odd):
                lane_at = slice(d * lanes, (d + 1) * lanes)
                c_here = jnp.broadcast_to(c_row[:, d : d + 1], (orb, lanes))
                s_here = jnp.broadcast_to(s_row[:, d : d + 1], (1, lanes)) * signs
                phased[i, at, lane_at] = (
                    placed[i, at, lane_at] * c_here + turned[i, at, lane_at] * s_here
                ).astype(BF16)
        return carry

    lax.fori_loop(0, pairs, phase, 0)

    out_signs = -signs
    inner_at, inner_end = reach, reach + atoms

    def dot(left, right):
        return jnp.dot(left, right, preferred_element_type=F32)

    def inner_products(k, c):
        par = k % 2
        for i in range(pairs):
            low, high = max(2 * i, inner_at), min(2 * i + wide, inner_end)
            inner[c, i * lanes : (i + 1) * lanes, :] = dot(
                phased[i, :, (low - 2 * i) * lanes : (high - 2 * i) * lanes],
                weights[par, c, low * lanes : high * lanes, :],
            )

    def take_halo(k, c, up_side):
        par = k % 2
        side = 1 if up_side else 0
        ok = has_up if up_side else has_down

        @pl.when(ok)
        def _():
            t_copy(k, c, not up_side).wait_recv()

        first = inner_end if up_side else 0
        for j in range(reach):
            value = halo[k, c, side, j * orb : (j + 1) * orb, :].astype(F32)
            value = jnp.where(ok, value, 0.0)
            base = (first + j) * lanes
            weights[par, c, base : base + orb, :] = value.astype(BF16)
            weights[par, c, base + orb : base + lanes, :] = (turn(value) * signs).astype(BF16)

    def finish_term(k, c):
        par = k % 2
        factor = elec_step / (k + 1)
        for up_side in (False, True):
            take_halo(k, c, up_side)
            for i in range(pairs // 2):
                if up_side:
                    i = i + pairs // 2
                    low, high = inner_end, 2 * i + wide
                else:
                    low, high = 2 * i, inner_at
                at = slice(i * lanes, (i + 1) * lanes)
                product = factor * (
                    inner[c, at, :]
                    + dot(
                        phased[i, :, (low - 2 * i) * lanes : (high - 2 * i) * lanes],
                        weights[par, c, low * lanes : high * lanes, :],
                    )
                )
                rotated = product.astype(BF16)
                value = (turn(product) * out_signs).astype(BF16)
                if k + 1 == TERMS and c + 1 == CHUNKS:
                    first = own[k + 1, 0, at, :].astype(F32)
                    second = value.astype(F32)
                    low = iota((1, lanes), 1) < orb
                    coef_out[0, at, :] = coef_out[0, at, :] + jnp.where(low, first, turn(second))
                    coef_out[1, at, :] = coef_out[1, at, :] + jnp.where(low, turn(first), second)
                    continue
                own[k + 1, c, at, :] = value
                if k + 1 < TERMS:
                    for j in range(2):
                        base = (inner_at + 2 * i + j) * lanes
                        part = slice(j * orb, (j + 1) * orb)
                        weights[1 - par, c, base : base + orb, :] = value[part]
                        weights[1 - par, c, base + orb : base + lanes, :] = rotated[part]

    def add_terms(which):
        def one(a, carry):
            at = pl.ds(pl.multiple_of(a * orb, orb), orb)
            first = sum(own[k, 0, at, :].astype(F32) for k in which)
            second = sum(own[k, 1, at, :].astype(F32) for k in which)
            coef_out[0, at, :] = coef_out[0, at, :] + jnp.where(low_lanes, first, turn(second))
            coef_out[1, at, :] = coef_out[1, at, :] + jnp.where(low_lanes, turn(first), second)
            return carry

        lax.fori_loop(0, atoms, one, 0)

    for c in range(CHUNKS):
        inner_products(0, c)
    for c in range(CHUNKS):
        finish_term(0, c)
        send_term(1, c)
        inner_products(1, c)

    def shares(i, carry):
        left = [vp[c, pl.ds(pl.multiple_of(i * lanes, lanes), lanes), :] for c in range(CHUNKS)]
        for d in range(0, wide, 2):
            base = pl.multiple_of(i * 2 * lanes + d * lanes, 2 * lanes)
            rows_at = pl.ds(base, 2 * lanes)
            gram = None
            for c in range(CHUNKS):
                product = lax.dot_general(
                    left[c], weights[0, c, rows_at, :], (((1,), (1,)), ((), ())),
                    preferred_element_type=F32,
                )
                gram = product if gram is None else gram + product
            gram = gram * phased[i, :, d * lanes : (d + 2) * lanes].astype(F32)
            for odd in range(2):
                summed = jnp.sum(gram[odd * orb : (odd + 1) * orb], axis=0, keepdims=True)
                for j in range(2):
                    share[2 * i + odd, d + j : d + j + 1, :] = summed[
                        :, j * lanes : (j + 1) * lanes
                    ]
        return carry

    share[...] = jnp.zeros(share.shape, F32)
    lax.fori_loop(0, pairs, shares, 0)
    scale = 1.0 / math.sqrt(2.0 * orb * groups * lanes)
    line = jnp.zeros(tile, F32)
    for a in range(atoms):
        each = jnp.sum(share[a], axis=1, keepdims=True)
        for c in range(3):
            bond = column(pos_rows[c], 1, 2 * (a // 2)) - pos_cols[c][a : a + 1, :]
            value = scale * jnp.sum(each * bond, axis=0, keepdims=True)
            line = line + jnp.where(lane1 == 4 * a + c, value, 0.0)
    cur_send[...] = line

    def cur_copy(i, slot, gg, rr):
        return pltpu.make_async_remote_copy(
            src_ref=cur_send, dst_ref=cur_recv.at[slot],
            send_sem=cur_ss.at[i], recv_sem=cur_rs.at[slot],
            device_id=device(gg, rr), device_id_type=MESH,
        )

    def for_cur_sends(action, keep):
        def one(i, carry):
            gg, rr = owner(per_row * r + i)
            is_self = (gg == g) & (rr == r)

            @pl.when(jnp.logical_not(is_self))
            def _():
                action(cur_copy(i, g, gg, rr))

            if keep:
                @pl.when(is_self)
                def _():
                    cur_recv[g] = cur_send[...]

            return carry

        lax.fori_loop(0, per_row, one, 0)

    for_cur_sends(lambda copy: copy.start(), True)

    @pl.when(has_prev)
    def _():
        e_copy.wait_send()

    @pl.when(has_next)
    def _():
        e_copy.wait_recv()

    comp = [field[c] for c in range(3)]
    ahead = [jnp.where(has_next, e_recv[c].astype(F32), 0.0) for c in range(2)]

    def ahead_y(v):
        return shifted(v, 0, True) - v

    def ahead_z(v):
        return shifted(v, 1, True) - v

    curl = (
        ahead_y(comp[2]) - ahead_z(comp[1]),
        ahead_z(comp[0]) - (ahead[1] - comp[2]),
        (ahead[0] - comp[1]) - ahead_y(comp[0]),
    )
    for c in range(3):
        field_out[3 + c] = field[3 + c] - wave_step * curl[c]
    for c in range(2):
        b_send[c] = field_out[4 + c].astype(BF16)

    @pl.when(has_next)
    def _():
        b_copy.start()

    for c in range(CHUNKS):
        finish_term(1, c)
        send_term(2, c)
        inner_products(2, c)
    add_terms((1, 2))

    @pl.when(has_next)
    def _():
        b_copy.wait_send()

    @pl.when(has_prev)
    def _():
        b_copy.wait_recv()

    def cur_wait(gg, carry):
        @pl.when((gg != g) | (q != r))
        def _():
            cur_copy(0, gg, gg, q).wait_recv()

        return carry

    lax.fori_loop(0, groups, cur_wait, 0)
    current = cur_recv[0]
    for gg in range(1, groups):
        current = current + cur_recv[gg]
    atom_one = first_here - atoms * q

    def picked(atom, c):
        return jnp.sum(jnp.where(lane1 == 4 * atom + c, current, 0.0), axis=1, keepdims=True)

    comp = [field_out[3 + c] for c in range(3)]
    behind = [jnp.where(has_prev, b_recv[c].astype(F32), 0.0) for c in range(2)]

    def behind_y(v):
        return v - shifted(v, 0, False)

    def behind_z(v):
        return v - shifted(v, 1, False)

    curl = (
        behind_y(comp[2]) - behind_z(comp[1]),
        behind_z(comp[0]) - (comp[2] - behind[1]),
        (comp[1] - behind[0]) - behind_y(comp[0]),
    )
    for c in range(3):
        source = jnp.where(at_one, picked(atom_one, c), 0.0) + jnp.where(
            at_two, picked(atom_one + 1, c), 0.0
        )
        electric = field[c] + wave_step * (curl[c] - source)
        field_out[c] = electric
        pot_out[c] = pot[c] - wave_step * electric

    stores = [
        pltpu.make_async_copy(source, target, out_sem.at[i])
        for i, (source, target) in enumerate(
            ((field_out, field_res), (pot_out, pot_res), (coef_out, coef_res))
        )
    ]
    stores[0].start()
    stores[1].start()

    for c in range(CHUNKS):
        finish_term(2, c)
    stores[2].start()

    for_at_sends(lambda copy: copy.wait_send(), False)
    for_cur_sends(lambda copy: copy.wait_send(), False)
    for k in range(TERMS):
        for c in range(CHUNKS):
            @pl.when(has_up)
            def _():
                t_copy(k, c, True).wait_send()

            @pl.when(has_down)
            def _():
                t_copy(k, c, False).wait_send()
    for store in stores:
        store.wait()


def hand_on(coef, field, pot, coef_out, field_out, pot_out, coef_buf, field_buf, pot_buf, in_sem, out_sem):
    half = coef.shape[1] // 2
    pieces = [(pot, pot_buf, pot_out)]
    for i in range(2):
        pieces.append([ref.at[pl.ds(3 * i, 3)] for ref in (field, field_buf, field_out)])
        for part in range(2):
            at = pl.ds(part * half, half)
            pieces.append([ref.at[i, at] for ref in (coef, coef_buf, coef_out)])
    loads, stores = [], []
    for i, piece in enumerate(pieces):
        source, held, target = piece
        loads.append(pltpu.make_async_copy(source, held, in_sem.at[i]))
        stores.append(pltpu.make_async_copy(held, target, out_sem.at[i]))
    for load in loads:
        load.start()
    for load, store in zip(loads, stores):
        load.wait()
        store.start()
    for store in stores:
        store.wait()


def body(groups, rows, coefficients, hamiltonian, neighbours, positions, atom_site, rs_field, potential):
    atoms, blocks, orb = hamiltonian.shape[:3]
    lanes = 2 * orb
    reach = atoms // 2
    pairs = atoms // 2
    wide = 2 * reach + 2
    per_row = groups
    grid = rs_field.shape[2:]
    own_rows = atoms * orb
    field_in = rs_field.reshape((6,) + grid)
    pot_in = potential.reshape((3,) + grid)
    dma = pltpu.SemaphoreType.DMA
    hbm = pl.BlockSpec(memory_space=pltpu.HBM)
    coef, field, pot = pl.pallas_call(
        functools.partial(kernel, groups, rows),
        out_shape=(
            jax.ShapeDtypeStruct(coefficients.shape, F32),
            jax.ShapeDtypeStruct(field_in.shape, F32),
            jax.ShapeDtypeStruct(pot_in.shape, F32),
        ),
        in_specs=[hbm] * 7,
        out_specs=(hbm, hbm, hbm),
        scratch_shapes=[
            pltpu.VMEM(coefficients.shape, F32),
            pltpu.VMEM(field_in.shape, F32),
            pltpu.VMEM(pot_in.shape, F32),
            pltpu.SMEM(neighbours.shape, jnp.int32),
            pltpu.VMEM(positions.shape, F32),
            pltpu.SMEM(atom_site.shape, jnp.int32),
            pltpu.VMEM(hamiltonian.shape, BF16),
            pltpu.VMEM((pairs, 2 * orb, wide * lanes), F32),
            pltpu.VMEM((pairs, 2 * orb, wide * lanes), F32),
            pltpu.VMEM((pairs, 2 * orb, wide * lanes), BF16),
            pltpu.VMEM((TERMS + 1, CHUNKS, own_rows, lanes), BF16),
            pltpu.VMEM((CHUNKS, own_rows, lanes), BF16),
            pltpu.VMEM((TERMS, CHUNKS, 2, reach * orb, lanes), BF16),
            pltpu.VMEM((2, CHUNKS, (atoms + 2 * reach) * lanes, lanes), BF16),
            pltpu.VMEM((CHUNKS, own_rows, lanes), F32),
            pltpu.VMEM(field_in.shape, F32),
            pltpu.VMEM(pot_in.shape, F32),
            pltpu.VMEM((2,) + grid, BF16),
            pltpu.VMEM((2,) + grid, BF16),
            pltpu.VMEM((2,) + grid, BF16),
            pltpu.VMEM((2,) + grid, BF16),
            pltpu.VMEM((2, 1, 128), F32),
            pltpu.VMEM((2 * per_row, 1, 128), F32),
            pltpu.VMEM((1, 128), F32),
            pltpu.VMEM((groups, 1, 128), F32),
            pltpu.VMEM((8, 512), F32),
            pltpu.VMEM((16, 128), F32),
            pltpu.VMEM((16, 128), F32),
            pltpu.VMEM((atoms, 16, 128), F32),
            dma((7,)),
            dma((3,)),
            dma((2, groups)),
            dma((2 * per_row,)),
            dma((per_row,)),
            dma((groups,)),
            dma((TERMS, CHUNKS, 2)),
            dma((TERMS, CHUNKS, 2)),
            dma((2,)),
            dma((2,)),
        ],
        compiler_params=pltpu.CompilerParams(
            collective_id=0, has_side_effects=True, vmem_limit_bytes=60 * 2**20
        ),
    )(coefficients, hamiltonian, neighbours, positions, atom_site, field_in, pot_in)
    coef, field, pot = pl.pallas_call(
        hand_on,
        out_shape=(
            jax.ShapeDtypeStruct(coefficients.shape, F32),
            jax.ShapeDtypeStruct(field_in.shape, F32),
            jax.ShapeDtypeStruct(pot_in.shape, F32),
        ),
        in_specs=[hbm, hbm, hbm],
        out_specs=(hbm, hbm, hbm),
        scratch_shapes=[
            pltpu.VMEM(coefficients.shape, F32),
            pltpu.VMEM(field_in.shape, F32),
            pltpu.VMEM(pot_in.shape, F32),
            dma((8,)),
            dma((8,)),
        ],
        compiler_params=pltpu.CompilerParams(vmem_limit_bytes=60 * 2**20),
    )(coef, field, pot)
    return coef, field.reshape(rs_field.shape), pot.reshape(potential.shape)


def solution(mesh):
    placed = (
        P(None, "row", "grp"),
        P("row", None, None, None),
        P("row", None),
        P(),
        P(),
        P(None, ("grp", "row"), None, None),
        P(None, ("grp", "row"), None, None),
    )
    return jax.shard_map(
        functools.partial(body, mesh.shape["grp"], mesh.shape["row"]),
        mesh=mesh,
        in_specs=placed,
        out_specs=(
            P(None, "row", "grp"),
            P(None, ("grp", "row"), None, None),
            P(None, ("grp", "row"), None, None),
        ),
        check_vma=False,
    )
```

```python
import functools
import math

import jax
import jax.numpy as jnp
from jax import lax
from jax.experimental import pallas as pl
from jax.experimental.pallas import tpu as pltpu
from jax.sharding import PartitionSpec as P

TERMS = 3
CHUNKS = 2

coupling = 0.7
elec_step = 1.5
wave_step = 0.5

MESH = pl.DeviceIdType.MESH
F32 = jnp.float32
BF16 = jnp.bfloat16


def iota(shape, dim):
    return lax.broadcasted_iota(jnp.int32, shape, dim)


def shifted(value, dim, forward):
    extent = value.shape[dim]
    moved = pltpu.roll(value, extent - 1 if forward else 1, dim)
    rim = extent - 1 if forward else 0
    return jnp.where(iota(value.shape, dim) == rim, 0.0, moved)


def kernel(
    groups, rows,
    coef_hbm, ham_hbm, nbr_hbm, pos_hbm, site_hbm, field_hbm, pot_hbm,
    coef_res, field_res, pot_res,
    coef_out, field_out, pot_out, nbr, pos, site, ham, placed, turned, phased, own, vp, halo, weights, inner,
    field, pot, e_send, e_recv, b_send, b_recv,
    at_send, at_recv, cur_send, cur_recv, posb, cos_tab, sin_tab, share,
    in_sem, out_sem, at_ss, at_rs, cur_ss, cur_rs, t_ss, t_rs, rim_ss, rim_rs,
):
    atoms = nbr.shape[0]
    blocks = nbr.shape[1]
    reach = atoms // 2
    orb = ham.shape[2]
    lanes = 2 * orb
    pairs = atoms // 2
    wide = 2 * reach + 2
    half_rows = reach * orb
    own_rows = atoms * orb
    atoms_all = pos.shape[1]
    planes = groups * rows
    per_row = planes // rows
    sources = 2 * per_row

    g = lax.axis_index("grp")
    r = lax.axis_index("row")
    s = g * rows + r
    q = lax.div(s, per_row)
    m = lax.rem(s, per_row)
    near = m < per_row // 2
    other = jnp.where(near, q - 1, q + 1)
    other_ok = (other >= 0) & (other < rows)

    def owner(p):
        return lax.div(p, rows), lax.rem(p, rows)

    def device(gg, rr):
        return {"grp": gg, "row": rr}

    next_g, next_r = owner(jnp.minimum(s + 1, planes - 1))
    prev_g, prev_r = owner(jnp.maximum(s - 1, 0))
    has_next, has_prev = s < planes - 1, s > 0
    has_up, has_down = r < rows - 1, r > 0

    loads = [
        pltpu.make_async_copy(source, target, in_sem.at[i])
        for i, (source, target) in enumerate((
            (pot_hbm, pot), (coef_hbm, coef_out), (ham_hbm, ham), (field_hbm, field),
            (site_hbm, site), (nbr_hbm, nbr), (pos_hbm, pos),
        ))
    ]
    for load in loads:
        load.start()

    barrier = pltpu.get_barrier_semaphore()

    def tell(gg, rr):
        pl.semaphore_signal(barrier, inc=1, device_id=device(gg, rr), device_id_type=MESH)

    first_plane = per_row * r - per_row // 2

    def tell_sources(i, carry):
        p = first_plane + i
        gg, rr = owner(jnp.clip(p, 0, planes - 1))

        @pl.when((p >= 0) & (p < planes) & ((gg != g) | (rr != r)))
        def _():
            tell(gg, rr)

        return carry

    def tell_currents(gg, carry):
        @pl.when((gg != g) | (q != r))
        def _():
            tell(gg, q)

        return carry

    @pl.when(has_next)
    def _():
        tell(next_g, next_r)

    @pl.when(has_prev)
    def _():
        tell(prev_g, prev_r)

    lax.fori_loop(0, sources, tell_sources, 0)

    loads[4].wait()
    first_here = lax.div(3 * s + 1, 2)
    second_ok = lax.rem(s, 2) == 0
    second_here = jnp.minimum(first_here + 1, atoms_all - 1)
    site_one = site[first_here]
    site_two = jnp.where(second_ok, site[second_here], -1)
    grid_y, grid_z = pot.shape[1], pot.shape[2]
    cell = iota((grid_y, grid_z), 0) * grid_z + iota((grid_y, grid_z), 1)
    at_one = cell == site_one
    at_two = cell == site_two
    tile = (1, 128)
    lane1 = iota(tile, 1)
    comp_step = 32

    loads[0].wait()
    found = []
    for mask in (at_one, at_two):
        for c in range(3):
            hit = jnp.sum(jnp.where(mask, pot[c], 0.0), axis=0, keepdims=True)
            found.append(jnp.sum(hit, axis=1, keepdims=True))
    for k, target in enumerate((q, other)):
        lane_one = first_here - atoms * target + reach
        message = jnp.zeros(tile, F32)
        for j in range(2):
            for c in range(3):
                message = message + jnp.where(
                    lane1 == lane_one + j + comp_step * c, found[3 * j + c], 0.0
                )
        at_send[k] = message

    low_lanes = iota((orb, lanes), 1) < orb
    half = lanes // 2

    def turn(value):
        return pltpu.roll(value, half, 1)

    loads[1].wait()

    def pack(a, carry):
        at = pl.ds(pl.multiple_of(a * orb, orb), orb)
        real = coef_out[0, at, :]
        imag = coef_out[1, at, :]
        real_turned, imag_turned = turn(real), turn(imag)
        first = jnp.where(low_lanes, real, imag_turned)
        first_other = jnp.where(low_lanes, -imag, real_turned)
        second = jnp.where(low_lanes, real_turned, imag)
        second_other = jnp.where(low_lanes, -imag_turned, real)
        for c, (value, rotated) in enumerate(((first, first_other), (second, second_other))):
            value = value.astype(BF16)
            rotated = rotated.astype(BF16)
            own[0, c, at, :] = value
            vp[c, at, :] = rotated
            base = pl.multiple_of((a + reach) * lanes, lanes)
            weights[0, c, pl.ds(base, orb), :] = value
            weights[0, c, pl.ds(base + orb, orb), :] = rotated
        return carry

    lax.fori_loop(0, atoms, pack, 0)

    loads[3].wait()
    for c in range(2):
        e_send[c] = field[1 + c].astype(BF16)

    loads[2].wait()
    loads[5].wait()
    zero_block = jnp.zeros((orb, lanes), F32)
    chunk_rows = 32

    def place(a, carry):
        i = lax.div(a, 2)
        odd = lax.rem(a, 2)
        offsets = [nbr[a, n] - atoms * r - a + reach for n in range(blocks)]

        def piece(part, inner_carry):
            at = pl.multiple_of(part * chunk_rows, chunk_rows)
            to = pl.ds(pl.multiple_of(odd * orb + at, chunk_rows), chunk_rows)
            held = [ham[a, n, pl.ds(at, chunk_rows), :].astype(F32) for n in range(blocks)]
            for d in range(wide - 1):
                who = list(range(3, blocks))
                if d == reach:
                    who = [0] + who
                if d == 0 or d == 2 * reach:
                    who = [1, 2] + who
                total = None
                for n in who:
                    scale = jnp.where(offsets[n] == d, 1.0, 0.0).astype(F32)
                    part_sum = held[n] * scale
                    total = part_sum if total is None else total + part_sum
                lane_at = pl.ds(pl.multiple_of((d + odd) * lanes, lanes), lanes)
                placed[i, to, lane_at] = total
                turned[i, to, lane_at] = turn(total)
            return inner_carry

        lax.fori_loop(0, orb // chunk_rows, piece, 0)
        return carry

    def ones(cond):
        return jnp.where(cond, 1, 0)

    expected = (
        groups
        + groups * ones(other_ok)
        - ones(q == r)
        - ones(other_ok & (other == r))
        + ones(has_next)
        + ones(has_prev)
    )
    pl.semaphore_wait(barrier, expected)

    def at_copy(k, slot, gg, rr):
        return pltpu.make_async_remote_copy(
            src_ref=at_send.at[k], dst_ref=at_recv.at[slot],
            send_sem=at_ss.at[k, gg], recv_sem=at_rs.at[slot],
            device_id=device(gg, rr), device_id_type=MESH,
        )

    slot_own = m + per_row // 2
    slot_other = jnp.where(near, m + per_row + per_row // 2, m - per_row // 2)

    def for_at_sends(action, keep):
        for k, (target, slot, ok) in enumerate(
            ((q, slot_own, None), (other, slot_other, other_ok))
        ):
            def one(gg, carry, k=k, target=target, slot=slot, ok=ok):
                is_self = (gg == g) & (target == r)
                go = jnp.logical_not(is_self)
                if ok is not None:
                    go = go & ok

                @pl.when(go)
                def _():
                    action(at_copy(k, slot, gg, target))

                if keep:
                    @pl.when(is_self)
                    def _():
                        at_recv[slot] = at_send[k]

                return carry

            lax.fori_loop(0, groups, one, 0)

    for_at_sends(lambda copy: copy.start(), True)

    def t_copy(k, c, up):
        side = 0 if up else 1
        source = pl.ds(own_rows - half_rows, half_rows) if up else pl.ds(0, half_rows)
        rr = next_r if up else prev_r
        return pltpu.make_async_remote_copy(
            src_ref=own.at[k, c, source, :], dst_ref=halo.at[k, c, side],
            send_sem=t_ss.at[k, c, side], recv_sem=t_rs.at[k, c, side],
            device_id=device(g, rr), device_id_type=MESH,
        )

    def send_side(k, c, up):
        @pl.when(has_up if up else has_down)
        def _():
            t_copy(k, c, up).start()

    def send_term(k, c):
        down_first = lax.rem(r, 4) == 0

        @pl.when(down_first & has_down)
        def _():
            t_copy(k, c, False).start()

        send_side(k, c, True)

        @pl.when(jnp.logical_not(down_first) & has_down)
        def _():
            t_copy(k, c, False).start()

    send_term(0, 0)

    e_copy = pltpu.make_async_remote_copy(
        src_ref=e_send, dst_ref=e_recv, send_sem=rim_ss.at[0], recv_sem=rim_rs.at[0],
        device_id=device(prev_g, prev_r), device_id_type=MESH,
    )
    b_copy = pltpu.make_async_remote_copy(
        src_ref=b_send, dst_ref=b_recv, send_sem=rim_ss.at[1], recv_sem=rim_rs.at[1],
        device_id=device(next_g, next_r), device_id_type=MESH,
    )

    lax.fori_loop(0, 6, place, 0)
    for c in range(1, CHUNKS):
        send_term(0, c)

    lax.fori_loop(6, atoms, place, 0)
    @pl.when(has_prev)
    def _():
        e_copy.start()

    for i in range(pairs):
        phased[i, 0:orb, (wide - 1) * lanes : wide * lanes] = zero_block.astype(BF16)
        phased[i, orb : 2 * orb, 0:lanes] = zero_block.astype(BF16)

    loads[6].wait()
    posb[...] = jnp.zeros(posb.shape, F32)
    posb[0:3, 0:atoms_all] = pos[...]
    shift = lax.rem(2 * posb.shape[1] + reach - atoms * r, posb.shape[1])
    near_pos = pltpu.roll(posb[...], shift, 1)[:, 0:128]
    sub16, lane16 = iota((16, 128), 0), iota((16, 128), 1)

    def column(row, step, offset):
        return jnp.sum(
            jnp.where(lane16 == step * sub16 + offset, row, 0.0), axis=1, keepdims=True
        )

    pos_rows = [near_pos[c : c + 1, :] for c in range(3)]
    pos_cols = [column(row, 1, reach) for row in pos_rows]

    def at_source(i):
        p = first_plane + i
        gg, rr = owner(jnp.clip(p, 0, planes - 1))
        return (p >= 0) & (p < planes), (gg == g) & (rr == r), gg, rr

    def at_wait(i, total):
        ok, is_self, gg, rr = at_source(i)

        @pl.when(ok & jnp.logical_not(is_self))
        def _():
            at_copy(0, i, gg, rr).wait_recv()

        return total

    lax.fori_loop(0, sources, at_wait, 0)
    at_near = jnp.zeros(tile, F32)
    for i in range(sources):
        ok = at_source(i)[0]
        at_near = at_near + jnp.where(ok, at_recv[i], 0.0)

    angle = jnp.zeros((16, 128), F32)
    for c in range(3):
        row = pltpu.roll(at_near, 128 - comp_step * c, 1) if c else at_near
        angle = angle + 0.5 * (column(row, 1, reach) + row) * (pos_rows[c] - pos_cols[c])
    angle = coupling * angle
    cosine, sine = jnp.cos(angle), jnp.sin(angle)
    for i in range(pairs):
        back = (128 - 2 * i) % 128
        c_rows, s_rows = cosine, sine
        if back:
            c_rows, s_rows = pltpu.roll(cosine, back, 1), pltpu.roll(sine, back, 1)
        cos_tab[2 * i : 2 * i + 2, :] = c_rows[2 * i : 2 * i + 2, :]
        sin_tab[2 * i : 2 * i + 2, :] = s_rows[2 * i : 2 * i + 2, :]

    signs = jnp.where(iota((1, lanes), 1) < orb, -1.0, 1.0).astype(F32)

    def phase(i, carry):
        for odd in range(2):
            c_row = cos_tab[pl.ds(2 * i + odd, 1), :]
            s_row = sin_tab[pl.ds(2 * i + odd, 1), :]
            at = slice(odd * orb, (odd + 1) * orb)
            for d in range(odd, wide - 1 + odd):
                lane_at = slice(d * lanes, (d + 1) * lanes)
                c_here = jnp.broadcast_to(c_row[:, d : d + 1], (orb, lanes))
                s_here = jnp.broadcast_to(s_row[:, d : d + 1], (1, lanes)) * signs
                phased[i, at, lane_at] = (
                    placed[i, at, lane_at] * c_here + turned[i, at, lane_at] * s_here
                ).astype(BF16)
        return carry

    lax.fori_loop(0, pairs, phase, 0)

    out_signs = -signs
    inner_at, inner_end = reach, reach + atoms

    def dot(left, right):
        return jnp.dot(left, right, preferred_element_type=F32)

    def inner_products(k, c):
        par = k % 2
        for i in range(pairs):
            low, high = max(2 * i, inner_at), min(2 * i + wide, inner_end)
            inner[c, i * lanes : (i + 1) * lanes, :] = dot(
                phased[i, :, (low - 2 * i) * lanes : (high - 2 * i) * lanes],
                weights[par, c, low * lanes : high * lanes, :],
            )

    def take_halo(k, c, up_side):
        par = k % 2
        side = 1 if up_side else 0
        ok = has_up if up_side else has_down

        @pl.when(ok)
        def _():
            t_copy(k, c, not up_side).wait_recv()

        first = inner_end if up_side else 0
        for j in range(reach):
            value = halo[k, c, side, j * orb : (j + 1) * orb, :].astype(F32)
            value = jnp.where(ok, value, 0.0)
            base = (first + j) * lanes
            weights[par, c, base : base + orb, :] = value.astype(BF16)
            weights[par, c, base + orb : base + lanes, :] = (turn(value) * signs).astype(BF16)

    def finish_term(k, c):
        par = k % 2
        factor = elec_step / (k + 1)
        for up_side in (True, False):
            take_halo(k, c, up_side)
            for i in range(pairs // 2):
                if up_side:
                    i = i + pairs // 2
                    low, high = inner_end, 2 * i + wide
                else:
                    low, high = 2 * i, inner_at
                at = slice(i * lanes, (i + 1) * lanes)
                product = factor * (
                    inner[c, at, :]
                    + dot(
                        phased[i, :, (low - 2 * i) * lanes : (high - 2 * i) * lanes],
                        weights[par, c, low * lanes : high * lanes, :],
                    )
                )
                rotated = product.astype(BF16)
                value = (turn(product) * out_signs).astype(BF16)
                if k + 1 == TERMS and c + 1 == CHUNKS:
                    first = own[k + 1, 0, at, :].astype(F32)
                    second = value.astype(F32)
                    low = iota((1, lanes), 1) < orb
                    coef_out[0, at, :] = coef_out[0, at, :] + jnp.where(low, first, turn(second))
                    coef_out[1, at, :] = coef_out[1, at, :] + jnp.where(low, turn(first), second)
                    continue
                own[k + 1, c, at, :] = value
                if k + 1 < TERMS:
                    for j in range(2):
                        base = (inner_at + 2 * i + j) * lanes
                        part = slice(j * orb, (j + 1) * orb)
                        weights[1 - par, c, base : base + orb, :] = value[part]
                        weights[1 - par, c, base + orb : base + lanes, :] = rotated[part]
            if k + 1 < TERMS:
                send_side(k + 1, c, up_side)

    def add_terms(which):
        def one(a, carry):
            at = pl.ds(pl.multiple_of(a * orb, orb), orb)
            first = sum(own[k, 0, at, :].astype(F32) for k in which)
            second = sum(own[k, 1, at, :].astype(F32) for k in which)
            coef_out[0, at, :] = coef_out[0, at, :] + jnp.where(low_lanes, first, turn(second))
            coef_out[1, at, :] = coef_out[1, at, :] + jnp.where(low_lanes, turn(first), second)
            return carry

        lax.fori_loop(0, atoms, one, 0)

    for c in range(CHUNKS):
        inner_products(0, c)
        finish_term(0, c)
    for c in range(CHUNKS):
        inner_products(1, c)

    def shares(i, carry):
        left = [vp[c, pl.ds(pl.multiple_of(i * lanes, lanes), lanes), :] for c in range(CHUNKS)]
        for d in range(0, wide, 2):
            base = pl.multiple_of(i * 2 * lanes + d * lanes, 2 * lanes)
            rows_at = pl.ds(base, 2 * lanes)
            gram = None
            for c in range(CHUNKS):
                product = lax.dot_general(
                    left[c], weights[0, c, rows_at, :], (((1,), (1,)), ((), ())),
                    preferred_element_type=F32,
                )
                gram = product if gram is None else gram + product
            gram = gram * phased[i, :, d * lanes : (d + 2) * lanes].astype(F32)
            for odd in range(2):
                summed = jnp.sum(gram[odd * orb : (odd + 1) * orb], axis=0, keepdims=True)
                for j in range(2):
                    share[2 * i + odd, d + j : d + j + 1, :] = summed[
                        :, j * lanes : (j + 1) * lanes
                    ]
        return carry

    share[...] = jnp.zeros(share.shape, F32)
    lax.fori_loop(0, pairs, shares, 0)
    scale = 1.0 / math.sqrt(2.0 * orb * groups * lanes)
    line = jnp.zeros(tile, F32)
    for a in range(atoms):
        each = jnp.sum(share[a], axis=1, keepdims=True)
        for c in range(3):
            bond = column(pos_rows[c], 1, 2 * (a // 2)) - pos_cols[c][a : a + 1, :]
            value = scale * jnp.sum(each * bond, axis=0, keepdims=True)
            line = line + jnp.where(lane1 == 4 * a + c, value, 0.0)
    cur_send[...] = line

    def cur_copy(i, slot, gg, rr):
        return pltpu.make_async_remote_copy(
            src_ref=cur_send, dst_ref=cur_recv.at[slot],
            send_sem=cur_ss.at[i], recv_sem=cur_rs.at[slot],
            device_id=device(gg, rr), device_id_type=MESH,
        )

    def for_cur_sends(action, keep):
        def one(i, carry):
            gg, rr = owner(per_row * r + i)
            is_self = (gg == g) & (rr == r)

            @pl.when(jnp.logical_not(is_self))
            def _():
                action(cur_copy(i, g, gg, rr))

            if keep:
                @pl.when(is_self)
                def _():
                    cur_recv[g] = cur_send[...]

            return carry

        lax.fori_loop(0, per_row, one, 0)

    for_cur_sends(lambda copy: copy.start(), True)

    @pl.when(has_prev)
    def _():
        e_copy.wait_send()

    @pl.when(has_next)
    def _():
        e_copy.wait_recv()

    comp = [field[c] for c in range(3)]
    ahead = [jnp.where(has_next, e_recv[c].astype(F32), 0.0) for c in range(2)]

    def ahead_y(v):
        return shifted(v, 0, True) - v

    def ahead_z(v):
        return shifted(v, 1, True) - v

    curl = (
        ahead_y(comp[2]) - ahead_z(comp[1]),
        ahead_z(comp[0]) - (ahead[1] - comp[2]),
        (ahead[0] - comp[1]) - ahead_y(comp[0]),
    )
    for c in range(3):
        field_out[3 + c] = field[3 + c] - wave_step * curl[c]
    for c in range(2):
        b_send[c] = field_out[4 + c].astype(BF16)

    @pl.when(has_next)
    def _():
        b_copy.start()

    for c in range(CHUNKS):
        finish_term(1, c)
        inner_products(2, c)
    add_terms((1, 2))

    @pl.when(has_next)
    def _():
        b_copy.wait_send()

    @pl.when(has_prev)
    def _():
        b_copy.wait_recv()

    def cur_wait(gg, carry):
        @pl.when((gg != g) | (q != r))
        def _():
            cur_copy(0, gg, gg, q).wait_recv()

        return carry

    lax.fori_loop(0, groups, cur_wait, 0)
    current = cur_recv[0]
    for gg in range(1, groups):
        current = current + cur_recv[gg]
    atom_one = first_here - atoms * q

    def picked(atom, c):
        return jnp.sum(jnp.where(lane1 == 4 * atom + c, current, 0.0), axis=1, keepdims=True)

    comp = [field_out[3 + c] for c in range(3)]
    behind = [jnp.where(has_prev, b_recv[c].astype(F32), 0.0) for c in range(2)]

    def behind_y(v):
        return v - shifted(v, 0, False)

    def behind_z(v):
        return v - shifted(v, 1, False)

    curl = (
        behind_y(comp[2]) - behind_z(comp[1]),
        behind_z(comp[0]) - (comp[2] - behind[1]),
        (comp[1] - behind[0]) - behind_y(comp[0]),
    )
    for c in range(3):
        source = jnp.where(at_one, picked(atom_one, c), 0.0) + jnp.where(
            at_two, picked(atom_one + 1, c), 0.0
        )
        electric = field[c] + wave_step * (curl[c] - source)
        field_out[c] = electric
        pot_out[c] = pot[c] - wave_step * electric

    stores = [
        pltpu.make_async_copy(source, target, out_sem.at[i])
        for i, (source, target) in enumerate(
            ((field_out, field_res), (pot_out, pot_res), (coef_out, coef_res))
        )
    ]
    stores[0].start()
    stores[1].start()

    for c in range(CHUNKS):
        finish_term(2, c)
    stores[2].start()

    for_at_sends(lambda copy: copy.wait_send(), False)
    for_cur_sends(lambda copy: copy.wait_send(), False)
    for k in range(TERMS):
        for c in range(CHUNKS):
            @pl.when(has_up)
            def _():
                t_copy(k, c, True).wait_send()

            @pl.when(has_down)
            def _():
                t_copy(k, c, False).wait_send()
    for store in stores:
        store.wait()


def hand_on(coef, field, pot, coef_out, field_out, pot_out, coef_buf, field_buf, pot_buf, in_sem, out_sem):
    half = coef.shape[1] // 2
    pieces = [(pot, pot_buf, pot_out)]
    for i in range(2):
        pieces.append([ref.at[pl.ds(3 * i, 3)] for ref in (field, field_buf, field_out)])
        for part in range(2):
            at = pl.ds(part * half, half)
            pieces.append([ref.at[i, at] for ref in (coef, coef_buf, coef_out)])
    loads, stores = [], []
    for i, piece in enumerate(pieces):
        source, held, target = piece
        loads.append(pltpu.make_async_copy(source, held, in_sem.at[i]))
        stores.append(pltpu.make_async_copy(held, target, out_sem.at[i]))
    for load in loads:
        load.start()
    for load, store in zip(loads, stores):
        load.wait()
        store.start()
    for store in stores:
        store.wait()


def body(groups, rows, coefficients, hamiltonian, neighbours, positions, atom_site, rs_field, potential):
    atoms, blocks, orb = hamiltonian.shape[:3]
    lanes = 2 * orb
    reach = atoms // 2
    pairs = atoms // 2
    wide = 2 * reach + 2
    per_row = groups
    grid = rs_field.shape[2:]
    own_rows = atoms * orb
    field_in = rs_field.reshape((6,) + grid)
    pot_in = potential.reshape((3,) + grid)
    dma = pltpu.SemaphoreType.DMA
    hbm = pl.BlockSpec(memory_space=pltpu.HBM)
    coef, field, pot = pl.pallas_call(
        functools.partial(kernel, groups, rows),
        out_shape=(
            jax.ShapeDtypeStruct(coefficients.shape, F32),
            jax.ShapeDtypeStruct(field_in.shape, F32),
            jax.ShapeDtypeStruct(pot_in.shape, F32),
        ),
        in_specs=[hbm] * 7,
        out_specs=(hbm, hbm, hbm),
        scratch_shapes=[
            pltpu.VMEM(coefficients.shape, F32),
            pltpu.VMEM(field_in.shape, F32),
            pltpu.VMEM(pot_in.shape, F32),
            pltpu.SMEM(neighbours.shape, jnp.int32),
            pltpu.VMEM(positions.shape, F32),
            pltpu.SMEM(atom_site.shape, jnp.int32),
            pltpu.VMEM(hamiltonian.shape, BF16),
            pltpu.VMEM((pairs, 2 * orb, wide * lanes), F32),
            pltpu.VMEM((pairs, 2 * orb, wide * lanes), F32),
            pltpu.VMEM((pairs, 2 * orb, wide * lanes), BF16),
            pltpu.VMEM((TERMS + 1, CHUNKS, own_rows, lanes), BF16),
            pltpu.VMEM((CHUNKS, own_rows, lanes), BF16),
            pltpu.VMEM((TERMS, CHUNKS, 2, reach * orb, lanes), BF16),
            pltpu.VMEM((2, CHUNKS, (atoms + 2 * reach) * lanes, lanes), BF16),
            pltpu.VMEM((CHUNKS, own_rows, lanes), F32),
            pltpu.VMEM(field_in.shape, F32),
            pltpu.VMEM(pot_in.shape, F32),
            pltpu.VMEM((2,) + grid, BF16),
            pltpu.VMEM((2,) + grid, BF16),
            pltpu.VMEM((2,) + grid, BF16),
            pltpu.VMEM((2,) + grid, BF16),
            pltpu.VMEM((2, 1, 128), F32),
            pltpu.VMEM((2 * per_row, 1, 128), F32),
            pltpu.VMEM((1, 128), F32),
            pltpu.VMEM((groups, 1, 128), F32),
            pltpu.VMEM((8, 512), F32),
            pltpu.VMEM((16, 128), F32),
            pltpu.VMEM((16, 128), F32),
            pltpu.VMEM((atoms, 16, 128), F32),
            dma((7,)),
            dma((3,)),
            dma((2, groups)),
            dma((2 * per_row,)),
            dma((per_row,)),
            dma((groups,)),
            dma((TERMS, CHUNKS, 2)),
            dma((TERMS, CHUNKS, 2)),
            dma((2,)),
            dma((2,)),
        ],
        compiler_params=pltpu.CompilerParams(
            collective_id=0, has_side_effects=True, vmem_limit_bytes=60 * 2**20
        ),
    )(coefficients, hamiltonian, neighbours, positions, atom_site, field_in, pot_in)
    coef, field, pot = pl.pallas_call(
        hand_on,
        out_shape=(
            jax.ShapeDtypeStruct(coefficients.shape, F32),
            jax.ShapeDtypeStruct(field_in.shape, F32),
            jax.ShapeDtypeStruct(pot_in.shape, F32),
        ),
        in_specs=[hbm, hbm, hbm],
        out_specs=(hbm, hbm, hbm),
        scratch_shapes=[
            pltpu.VMEM(coefficients.shape, F32),
            pltpu.VMEM(field_in.shape, F32),
            pltpu.VMEM(pot_in.shape, F32),
            dma((8,)),
            dma((8,)),
        ],
        compiler_params=pltpu.CompilerParams(vmem_limit_bytes=60 * 2**20),
    )(coef, field, pot)
    return coef, field.reshape(rs_field.shape), pot.reshape(potential.shape)


def solution(mesh):
    placed = (
        P(None, "row", "grp"),
        P("row", None, None, None),
        P("row", None),
        P(),
        P(),
        P(None, ("grp", "row"), None, None),
        P(None, ("grp", "row"), None, None),
    )
    return jax.shard_map(
        functools.partial(body, mesh.shape["grp"], mesh.shape["row"]),
        mesh=mesh,
        in_specs=placed,
        out_specs=(
            P(None, "row", "grp"),
            P(None, ("grp", "row"), None, None),
            P(None, ("grp", "row"), None, None),
        ),
        check_vma=False,
    )
```

```python
import functools
import math

import jax
import jax.numpy as jnp
from jax import lax
from jax.experimental import pallas as pl
from jax.experimental.pallas import tpu as pltpu
from jax.sharding import PartitionSpec as P

TERMS = 3
CHUNKS = 2

coupling = 0.7
elec_step = 1.5
wave_step = 0.5

MESH = pl.DeviceIdType.MESH
F32 = jnp.float32
BF16 = jnp.bfloat16


def iota(shape, dim):
    return lax.broadcasted_iota(jnp.int32, shape, dim)


def shifted(value, dim, forward):
    extent = value.shape[dim]
    moved = pltpu.roll(value, extent - 1 if forward else 1, dim)
    rim = extent - 1 if forward else 0
    return jnp.where(iota(value.shape, dim) == rim, 0.0, moved)


def kernel(
    groups, rows,
    coef_hbm, ham_hbm, nbr_hbm, pos_hbm, site_hbm, field_hbm, pot_hbm,
    coef_res, field_res, pot_res,
    coef_out, field_out, pot_out, nbr, pos, site, ham, placed, turned, phased, own, vp, halo, weights, inner,
    field, pot, e_send, e_recv, b_send, b_recv,
    at_send, at_recv, cur_send, cur_recv, posb, cos_tab, sin_tab, share,
    in_sem, out_sem, at_ss, at_rs, cur_ss, cur_rs, t_ss, t_rs, rim_ss, rim_rs,
):
    atoms = nbr.shape[0]
    blocks = nbr.shape[1]
    reach = atoms // 2
    orb = ham.shape[2]
    lanes = 2 * orb
    pairs = atoms // 2
    wide = 2 * reach + 2
    half_rows = reach * orb
    own_rows = atoms * orb
    atoms_all = pos.shape[1]
    planes = groups * rows
    per_row = planes // rows
    sources = 2 * per_row

    g = lax.axis_index("grp")
    r = lax.axis_index("row")
    s = g * rows + r
    q = lax.div(s, per_row)
    m = lax.rem(s, per_row)
    near = m < per_row // 2
    other = jnp.where(near, q - 1, q + 1)
    other_ok = (other >= 0) & (other < rows)

    def owner(p):
        return lax.div(p, rows), lax.rem(p, rows)

    def device(gg, rr):
        return {"grp": gg, "row": rr}

    next_g, next_r = owner(jnp.minimum(s + 1, planes - 1))
    prev_g, prev_r = owner(jnp.maximum(s - 1, 0))
    has_next, has_prev = s < planes - 1, s > 0
    has_up, has_down = r < rows - 1, r > 0

    loads = [
        pltpu.make_async_copy(source, target, in_sem.at[i])
        for i, (source, target) in enumerate((
            (pot_hbm, pot), (coef_hbm, coef_out), (ham_hbm, ham), (field_hbm, field),
            (site_hbm, site), (nbr_hbm, nbr), (pos_hbm, pos),
        ))
    ]
    for load in loads:
        load.start()

    barrier = pltpu.get_barrier_semaphore()

    def tell(gg, rr):
        pl.semaphore_signal(barrier, inc=1, device_id=device(gg, rr), device_id_type=MESH)

    first_plane = per_row * r - per_row // 2

    def tell_sources(i, carry):
        p = first_plane + i
        gg, rr = owner(jnp.clip(p, 0, planes - 1))

        @pl.when((p >= 0) & (p < planes) & ((gg != g) | (rr != r)))
        def _():
            tell(gg, rr)

        return carry

    def tell_currents(gg, carry):
        @pl.when((gg != g) | (q != r))
        def _():
            tell(gg, q)

        return carry

    @pl.when(has_next)
    def _():
        tell(next_g, next_r)

    @pl.when(has_prev)
    def _():
        tell(prev_g, prev_r)

    lax.fori_loop(0, sources, tell_sources, 0, unroll=4)

    loads[4].wait()
    first_here = lax.div(3 * s + 1, 2)
    second_ok = lax.rem(s, 2) == 0
    second_here = jnp.minimum(first_here + 1, atoms_all - 1)
    site_one = site[first_here]
    site_two = jnp.where(second_ok, site[second_here], -1)
    grid_y, grid_z = pot.shape[1], pot.shape[2]
    cell = iota((grid_y, grid_z), 0) * grid_z + iota((grid_y, grid_z), 1)
    at_one = cell == site_one
    at_two = cell == site_two
    tile = (1, 128)
    lane1 = iota(tile, 1)
    comp_step = 32

    loads[0].wait()
    found = []
    for mask in (at_one, at_two):
        for c in range(3):
            hit = jnp.sum(jnp.where(mask, pot[c], 0.0), axis=0, keepdims=True)
            found.append(jnp.sum(hit, axis=1, keepdims=True))
    for k, target in enumerate((q, other)):
        lane_one = first_here - atoms * target + reach
        message = jnp.zeros(tile, F32)
        for j in range(2):
            for c in range(3):
                message = message + jnp.where(
                    lane1 == lane_one + j + comp_step * c, found[3 * j + c], 0.0
                )
        at_send[k] = message

    low_lanes = iota((orb, lanes), 1) < orb
    half = lanes // 2

    def turn(value):
        return pltpu.roll(value, half, 1)

    loads[1].wait()

    def pack(a, carry):
        at = pl.ds(pl.multiple_of(a * orb, orb), orb)
        real = coef_out[0, at, :]
        imag = coef_out[1, at, :]
        real_turned, imag_turned = turn(real), turn(imag)
        first = jnp.where(low_lanes, real, imag_turned)
        first_other = jnp.where(low_lanes, -imag, real_turned)
        second = jnp.where(low_lanes, real_turned, imag)
        second_other = jnp.where(low_lanes, -imag_turned, real)
        for c, (value, rotated) in enumerate(((first, first_other), (second, second_other))):
            value = value.astype(BF16)
            rotated = rotated.astype(BF16)
            own[0, c, at, :] = value
            vp[c, at, :] = rotated
            base = pl.multiple_of((a + reach) * lanes, lanes)
            weights[0, c, pl.ds(base, orb), :] = value
            weights[0, c, pl.ds(base + orb, orb), :] = rotated
        return carry

    lax.fori_loop(0, atoms, pack, 0)

    loads[3].wait()
    for c in range(2):
        e_send[c] = field[1 + c].astype(BF16)

    loads[2].wait()
    loads[5].wait()
    zero_block = jnp.zeros((orb, lanes), F32)
    chunk_rows = 32

    def place(a, carry):
        i = lax.div(a, 2)
        odd = lax.rem(a, 2)
        offsets = [nbr[a, n] - atoms * r - a + reach for n in range(blocks)]

        def piece(part, inner_carry):
            at = pl.multiple_of(part * chunk_rows, chunk_rows)
            to = pl.ds(pl.multiple_of(odd * orb + at, chunk_rows), chunk_rows)
            held = [ham[a, n, pl.ds(at, chunk_rows), :].astype(F32) for n in range(blocks)]
            for d in range(wide - 1):
                who = list(range(3, blocks))
                if d == reach:
                    who = [0] + who
                if d == 0 or d == 2 * reach:
                    who = [1, 2] + who
                total = None
                for n in who:
                    scale = jnp.where(offsets[n] == d, 1.0, 0.0).astype(F32)
                    part_sum = held[n] * scale
                    total = part_sum if total is None else total + part_sum
                lane_at = pl.ds(pl.multiple_of((d + odd) * lanes, lanes), lanes)
                placed[i, to, lane_at] = total
                turned[i, to, lane_at] = turn(total)
            return inner_carry

        lax.fori_loop(0, orb // chunk_rows, piece, 0)
        return carry

    def ones(cond):
        return jnp.where(cond, 1, 0)

    expected = (
        groups
        + groups * ones(other_ok)
        - ones(q == r)
        - ones(other_ok & (other == r))
        + ones(has_next)
        + ones(has_prev)
    )
    pl.semaphore_wait(barrier, expected)

    def at_copy(k, slot, gg, rr):
        return pltpu.make_async_remote_copy(
            src_ref=at_send.at[k], dst_ref=at_recv.at[slot],
            send_sem=at_ss.at[k, gg], recv_sem=at_rs.at[slot],
            device_id=device(gg, rr), device_id_type=MESH,
        )

    slot_own = m + per_row // 2
    slot_other = jnp.where(near, m + per_row + per_row // 2, m - per_row // 2)

    def for_at_sends(action, keep):
        for k, (target, slot, ok) in enumerate(
            ((q, slot_own, None), (other, slot_other, other_ok))
        ):
            def one(gg, carry, k=k, target=target, slot=slot, ok=ok):
                is_self = (gg == g) & (target == r)
                go = jnp.logical_not(is_self)
                if ok is not None:
                    go = go & ok

                @pl.when(go)
                def _():
                    action(at_copy(k, slot, gg, target))

                if keep:
                    @pl.when(is_self)
                    def _():
                        at_recv[slot] = at_send[k]

                return carry

            lax.fori_loop(0, groups, one, 0, unroll=4)

    for_at_sends(lambda copy: copy.start(), True)

    def t_copy(k, c, up):
        side = 0 if up else 1
        source = pl.ds(own_rows - half_rows, half_rows) if up else pl.ds(0, half_rows)
        rr = next_r if up else prev_r
        return pltpu.make_async_remote_copy(
            src_ref=own.at[k, c, source, :], dst_ref=halo.at[k, c, side],
            send_sem=t_ss.at[k, c, side], recv_sem=t_rs.at[k, c, side],
            device_id=device(g, rr), device_id_type=MESH,
        )

    def send_side(k, c, up):
        @pl.when(has_up if up else has_down)
        def _():
            t_copy(k, c, up).start()

    def send_term(k, c):
        down_first = lax.rem(r, 4) == 0

        @pl.when(down_first & has_down)
        def _():
            t_copy(k, c, False).start()

        send_side(k, c, True)

        @pl.when(jnp.logical_not(down_first) & has_down)
        def _():
            t_copy(k, c, False).start()

    send_term(0, 0)

    e_copy = pltpu.make_async_remote_copy(
        src_ref=e_send, dst_ref=e_recv, send_sem=rim_ss.at[0], recv_sem=rim_rs.at[0],
        device_id=device(prev_g, prev_r), device_id_type=MESH,
    )
    b_copy = pltpu.make_async_remote_copy(
        src_ref=b_send, dst_ref=b_recv, send_sem=rim_ss.at[1], recv_sem=rim_rs.at[1],
        device_id=device(next_g, next_r), device_id_type=MESH,
    )

    lax.fori_loop(0, 6, place, 0)
    for c in range(1, CHUNKS):
        send_term(0, c)

    lax.fori_loop(6, atoms, place, 0)
    @pl.when(has_prev)
    def _():
        e_copy.start()

    for i in range(pairs):
        phased[i, 0:orb, (wide - 1) * lanes : wide * lanes] = zero_block.astype(BF16)
        phased[i, orb : 2 * orb, 0:lanes] = zero_block.astype(BF16)

    loads[6].wait()
    posb[...] = jnp.zeros(posb.shape, F32)
    posb[0:3, 0:atoms_all] = pos[...]
    shift = lax.rem(2 * posb.shape[1] + reach - atoms * r, posb.shape[1])
    near_pos = pltpu.roll(posb[...], shift, 1)[:, 0:128]
    sub16, lane16 = iota((16, 128), 0), iota((16, 128), 1)

    def column(row, step, offset):
        return jnp.sum(
            jnp.where(lane16 == step * sub16 + offset, row, 0.0), axis=1, keepdims=True
        )

    pos_rows = [near_pos[c : c + 1, :] for c in range(3)]
    pos_cols = [column(row, 1, reach) for row in pos_rows]

    def at_source(i):
        p = first_plane + i
        gg, rr = owner(jnp.clip(p, 0, planes - 1))
        return (p >= 0) & (p < planes), (gg == g) & (rr == r), gg, rr

    def at_wait(i, total):
        ok, is_self, gg, rr = at_source(i)

        @pl.when(ok & jnp.logical_not(is_self))
        def _():
            at_copy(0, i, gg, rr).wait_recv()

        return total

    lax.fori_loop(0, sources, at_wait, 0)
    at_near = jnp.zeros(tile, F32)
    for i in range(sources):
        ok = at_source(i)[0]
        at_near = at_near + jnp.where(ok, at_recv[i], 0.0)

    angle = jnp.zeros((16, 128), F32)
    for c in range(3):
        row = pltpu.roll(at_near, 128 - comp_step * c, 1) if c else at_near
        angle = angle + 0.5 * (column(row, 1, reach) + row) * (pos_rows[c] - pos_cols[c])
    angle = coupling * angle
    cosine, sine = jnp.cos(angle), jnp.sin(angle)
    for i in range(pairs):
        back = (128 - 2 * i) % 128
        c_rows, s_rows = cosine, sine
        if back:
            c_rows, s_rows = pltpu.roll(cosine, back, 1), pltpu.roll(sine, back, 1)
        cos_tab[2 * i : 2 * i + 2, :] = c_rows[2 * i : 2 * i + 2, :]
        sin_tab[2 * i : 2 * i + 2, :] = s_rows[2 * i : 2 * i + 2, :]

    signs = jnp.where(iota((1, lanes), 1) < orb, -1.0, 1.0).astype(F32)

    def phase(i, carry):
        for odd in range(2):
            c_row = cos_tab[pl.ds(2 * i + odd, 1), :]
            s_row = sin_tab[pl.ds(2 * i + odd, 1), :]
            at = slice(odd * orb, (odd + 1) * orb)
            for d in range(odd, wide - 1 + odd):
                lane_at = slice(d * lanes, (d + 1) * lanes)
                c_here = jnp.broadcast_to(c_row[:, d : d + 1], (orb, lanes))
                s_here = jnp.broadcast_to(s_row[:, d : d + 1], (1, lanes)) * signs
                phased[i, at, lane_at] = (
                    placed[i, at, lane_at] * c_here + turned[i, at, lane_at] * s_here
                ).astype(BF16)
        return carry

    lax.fori_loop(0, pairs, phase, 0)

    out_signs = -signs
    inner_at, inner_end = reach, reach + atoms

    def dot(left, right):
        return jnp.dot(left, right, preferred_element_type=F32)

    def inner_products(k, c):
        par = k % 2
        for i in range(pairs):
            low, high = max(2 * i, inner_at), min(2 * i + wide, inner_end)
            inner[c, i * lanes : (i + 1) * lanes, :] = dot(
                phased[i, :, (low - 2 * i) * lanes : (high - 2 * i) * lanes],
                weights[par, c, low * lanes : high * lanes, :],
            )

    def take_halo(k, c, up_side):
        par = k % 2
        side = 1 if up_side else 0
        ok = has_up if up_side else has_down

        @pl.when(ok)
        def _():
            t_copy(k, c, not up_side).wait_recv()

        first = inner_end if up_side else 0
        for j in range(reach):
            value = halo[k, c, side, j * orb : (j + 1) * orb, :].astype(F32)
            value = jnp.where(ok, value, 0.0)
            base = (first + j) * lanes
            weights[par, c, base : base + orb, :] = value.astype(BF16)
            weights[par, c, base + orb : base + lanes, :] = (turn(value) * signs).astype(BF16)

    def finish_term(k, c):
        par = k % 2
        factor = elec_step / (k + 1)
        for up_side in (True, False):
            take_halo(k, c, up_side)
            for i in range(pairs // 2):
                if up_side:
                    i = i + pairs // 2
                    low, high = inner_end, 2 * i + wide
                else:
                    low, high = 2 * i, inner_at
                at = slice(i * lanes, (i + 1) * lanes)
                product = factor * (
                    inner[c, at, :]
                    + dot(
                        phased[i, :, (low - 2 * i) * lanes : (high - 2 * i) * lanes],
                        weights[par, c, low * lanes : high * lanes, :],
                    )
                )
                rotated = product.astype(BF16)
                value = (turn(product) * out_signs).astype(BF16)
                if k + 1 == TERMS and c + 1 == CHUNKS:
                    first = own[k + 1, 0, at, :].astype(F32)
                    second = value.astype(F32)
                    low = iota((1, lanes), 1) < orb
                    coef_out[0, at, :] = coef_out[0, at, :] + jnp.where(low, first, turn(second))
                    coef_out[1, at, :] = coef_out[1, at, :] + jnp.where(low, turn(first), second)
                    continue
                own[k + 1, c, at, :] = value
                if k + 1 < TERMS:
                    for j in range(2):
                        base = (inner_at + 2 * i + j) * lanes
                        part = slice(j * orb, (j + 1) * orb)
                        weights[1 - par, c, base : base + orb, :] = value[part]
                        weights[1 - par, c, base + orb : base + lanes, :] = rotated[part]
            if k + 1 < TERMS:
                send_side(k + 1, c, up_side)

    def add_terms(which):
        def one(a, carry):
            at = pl.ds(pl.multiple_of(a * orb, orb), orb)
            first = sum(own[k, 0, at, :].astype(F32) for k in which)
            second = sum(own[k, 1, at, :].astype(F32) for k in which)
            coef_out[0, at, :] = coef_out[0, at, :] + jnp.where(low_lanes, first, turn(second))
            coef_out[1, at, :] = coef_out[1, at, :] + jnp.where(low_lanes, turn(first), second)
            return carry

        lax.fori_loop(0, atoms, one, 0)

    for c in range(CHUNKS):
        inner_products(0, c)
        finish_term(0, c)
    for c in range(CHUNKS):
        inner_products(1, c)

    def shares(i, carry):
        left = [vp[c, pl.ds(pl.multiple_of(i * lanes, lanes), lanes), :] for c in range(CHUNKS)]
        for d in range(0, wide, 2):
            base = pl.multiple_of(i * 2 * lanes + d * lanes, 2 * lanes)
            rows_at = pl.ds(base, 2 * lanes)
            gram = None
            for c in range(CHUNKS):
                product = lax.dot_general(
                    left[c], weights[0, c, rows_at, :], (((1,), (1,)), ((), ())),
                    preferred_element_type=F32,
                )
                gram = product if gram is None else gram + product
            gram = gram * phased[i, :, d * lanes : (d + 2) * lanes].astype(F32)
            for odd in range(2):
                summed = jnp.sum(gram[odd * orb : (odd + 1) * orb], axis=0, keepdims=True)
                for j in range(2):
                    share[2 * i + odd, d + j : d + j + 1, :] = summed[
                        :, j * lanes : (j + 1) * lanes
                    ]
        return carry

    share[...] = jnp.zeros(share.shape, F32)
    lax.fori_loop(0, pairs, shares, 0)
    scale = 1.0 / math.sqrt(2.0 * orb * groups * lanes)
    line = jnp.zeros(tile, F32)
    for a in range(atoms):
        each = jnp.sum(share[a], axis=1, keepdims=True)
        for c in range(3):
            bond = column(pos_rows[c], 1, 2 * (a // 2)) - pos_cols[c][a : a + 1, :]
            value = scale * jnp.sum(each * bond, axis=0, keepdims=True)
            line = line + jnp.where(lane1 == 4 * a + c, value, 0.0)
    cur_send[...] = line

    def cur_copy(i, slot, gg, rr):
        return pltpu.make_async_remote_copy(
            src_ref=cur_send, dst_ref=cur_recv.at[slot],
            send_sem=cur_ss.at[i], recv_sem=cur_rs.at[slot],
            device_id=device(gg, rr), device_id_type=MESH,
        )

    def for_cur_sends(action, keep):
        def one(i, carry):
            gg, rr = owner(per_row * r + i)
            is_self = (gg == g) & (rr == r)

            @pl.when(jnp.logical_not(is_self))
            def _():
                action(cur_copy(i, g, gg, rr))

            if keep:
                @pl.when(is_self)
                def _():
                    cur_recv[g] = cur_send[...]

            return carry

        lax.fori_loop(0, per_row, one, 0)

    for_cur_sends(lambda copy: copy.start(), True)

    @pl.when(has_prev)
    def _():
        e_copy.wait_send()

    @pl.when(has_next)
    def _():
        e_copy.wait_recv()

    comp = [field[c] for c in range(3)]
    ahead = [jnp.where(has_next, e_recv[c].astype(F32), 0.0) for c in range(2)]

    def ahead_y(v):
        return shifted(v, 0, True) - v

    def ahead_z(v):
        return shifted(v, 1, True) - v

    curl = (
        ahead_y(comp[2]) - ahead_z(comp[1]),
        ahead_z(comp[0]) - (ahead[1] - comp[2]),
        (ahead[0] - comp[1]) - ahead_y(comp[0]),
    )
    for c in range(3):
        field_out[3 + c] = field[3 + c] - wave_step * curl[c]
    for c in range(2):
        b_send[c] = field_out[4 + c].astype(BF16)

    @pl.when(has_next)
    def _():
        b_copy.start()

    for c in range(CHUNKS):
        finish_term(1, c)
        inner_products(2, c)
    add_terms((1, 2))

    @pl.when(has_next)
    def _():
        b_copy.wait_send()

    @pl.when(has_prev)
    def _():
        b_copy.wait_recv()

    def cur_wait(gg, carry):
        @pl.when((gg != g) | (q != r))
        def _():
            cur_copy(0, gg, gg, q).wait_recv()

        return carry

    lax.fori_loop(0, groups, cur_wait, 0)
    current = cur_recv[0]
    for gg in range(1, groups):
        current = current + cur_recv[gg]
    atom_one = first_here - atoms * q

    def picked(atom, c):
        return jnp.sum(jnp.where(lane1 == 4 * atom + c, current, 0.0), axis=1, keepdims=True)

    comp = [field_out[3 + c] for c in range(3)]
    behind = [jnp.where(has_prev, b_recv[c].astype(F32), 0.0) for c in range(2)]

    def behind_y(v):
        return v - shifted(v, 0, False)

    def behind_z(v):
        return v - shifted(v, 1, False)

    curl = (
        behind_y(comp[2]) - behind_z(comp[1]),
        behind_z(comp[0]) - (comp[2] - behind[1]),
        (comp[1] - behind[0]) - behind_y(comp[0]),
    )
    for c in range(3):
        source = jnp.where(at_one, picked(atom_one, c), 0.0) + jnp.where(
            at_two, picked(atom_one + 1, c), 0.0
        )
        electric = field[c] + wave_step * (curl[c] - source)
        field_out[c] = electric
        pot_out[c] = pot[c] - wave_step * electric

    stores = [
        pltpu.make_async_copy(source, target, out_sem.at[i])
        for i, (source, target) in enumerate(
            ((field_out, field_res), (pot_out, pot_res), (coef_out, coef_res))
        )
    ]
    stores[0].start()
    stores[1].start()

    for c in range(CHUNKS):
        finish_term(2, c)
    stores[2].start()

    for_at_sends(lambda copy: copy.wait_send(), False)
    for_cur_sends(lambda copy: copy.wait_send(), False)
    for k in range(TERMS):
        for c in range(CHUNKS):
            @pl.when(has_up)
            def _():
                t_copy(k, c, True).wait_send()

            @pl.when(has_down)
            def _():
                t_copy(k, c, False).wait_send()
    for store in stores:
        store.wait()


def hand_on(coef, field, pot, coef_out, field_out, pot_out, coef_buf, field_buf, pot_buf, in_sem, out_sem):
    half = coef.shape[1] // 2
    pieces = [(pot, pot_buf, pot_out)]
    for i in range(2):
        pieces.append([ref.at[pl.ds(3 * i, 3)] for ref in (field, field_buf, field_out)])
        for part in range(2):
            at = pl.ds(part * half, half)
            pieces.append([ref.at[i, at] for ref in (coef, coef_buf, coef_out)])
    loads, stores = [], []
    for i, piece in enumerate(pieces):
        source, held, target = piece
        loads.append(pltpu.make_async_copy(source, held, in_sem.at[i]))
        stores.append(pltpu.make_async_copy(held, target, out_sem.at[i]))
    for load in loads:
        load.start()
    for load, store in zip(loads, stores):
        load.wait()
        store.start()
    for store in stores:
        store.wait()


def body(groups, rows, coefficients, hamiltonian, neighbours, positions, atom_site, rs_field, potential):
    atoms, blocks, orb = hamiltonian.shape[:3]
    lanes = 2 * orb
    reach = atoms // 2
    pairs = atoms // 2
    wide = 2 * reach + 2
    per_row = groups
    grid = rs_field.shape[2:]
    own_rows = atoms * orb
    field_in = rs_field.reshape((6,) + grid)
    pot_in = potential.reshape((3,) + grid)
    dma = pltpu.SemaphoreType.DMA
    hbm = pl.BlockSpec(memory_space=pltpu.HBM)
    coef, field, pot = pl.pallas_call(
        functools.partial(kernel, groups, rows),
        out_shape=(
            jax.ShapeDtypeStruct(coefficients.shape, F32),
            jax.ShapeDtypeStruct(field_in.shape, F32),
            jax.ShapeDtypeStruct(pot_in.shape, F32),
        ),
        in_specs=[hbm] * 7,
        out_specs=(hbm, hbm, hbm),
        scratch_shapes=[
            pltpu.VMEM(coefficients.shape, F32),
            pltpu.VMEM(field_in.shape, F32),
            pltpu.VMEM(pot_in.shape, F32),
            pltpu.SMEM(neighbours.shape, jnp.int32),
            pltpu.VMEM(positions.shape, F32),
            pltpu.SMEM(atom_site.shape, jnp.int32),
            pltpu.VMEM(hamiltonian.shape, BF16),
            pltpu.VMEM((pairs, 2 * orb, wide * lanes), F32),
            pltpu.VMEM((pairs, 2 * orb, wide * lanes), F32),
            pltpu.VMEM((pairs, 2 * orb, wide * lanes), BF16),
            pltpu.VMEM((TERMS + 1, CHUNKS, own_rows, lanes), BF16),
            pltpu.VMEM((CHUNKS, own_rows, lanes), BF16),
            pltpu.VMEM((TERMS, CHUNKS, 2, reach * orb, lanes), BF16),
            pltpu.VMEM((2, CHUNKS, (atoms + 2 * reach) * lanes, lanes), BF16),
            pltpu.VMEM((CHUNKS, own_rows, lanes), F32),
            pltpu.VMEM(field_in.shape, F32),
            pltpu.VMEM(pot_in.shape, F32),
            pltpu.VMEM((2,) + grid, BF16),
            pltpu.VMEM((2,) + grid, BF16),
            pltpu.VMEM((2,) + grid, BF16),
            pltpu.VMEM((2,) + grid, BF16),
            pltpu.VMEM((2, 1, 128), F32),
            pltpu.VMEM((2 * per_row, 1, 128), F32),
            pltpu.VMEM((1, 128), F32),
            pltpu.VMEM((groups, 1, 128), F32),
            pltpu.VMEM((8, 512), F32),
            pltpu.VMEM((16, 128), F32),
            pltpu.VMEM((16, 128), F32),
            pltpu.VMEM((atoms, 16, 128), F32),
            dma((7,)),
            dma((3,)),
            dma((2, groups)),
            dma((2 * per_row,)),
            dma((per_row,)),
            dma((groups,)),
            dma((TERMS, CHUNKS, 2)),
            dma((TERMS, CHUNKS, 2)),
            dma((2,)),
            dma((2,)),
        ],
        compiler_params=pltpu.CompilerParams(
            collective_id=0, has_side_effects=True, vmem_limit_bytes=60 * 2**20
        ),
    )(coefficients, hamiltonian, neighbours, positions, atom_site, field_in, pot_in)
    coef, field, pot = pl.pallas_call(
        hand_on,
        out_shape=(
            jax.ShapeDtypeStruct(coefficients.shape, F32),
            jax.ShapeDtypeStruct(field_in.shape, F32),
            jax.ShapeDtypeStruct(pot_in.shape, F32),
        ),
        in_specs=[hbm, hbm, hbm],
        out_specs=(hbm, hbm, hbm),
        scratch_shapes=[
            pltpu.VMEM(coefficients.shape, F32),
            pltpu.VMEM(field_in.shape, F32),
            pltpu.VMEM(pot_in.shape, F32),
            dma((8,)),
            dma((8,)),
        ],
        compiler_params=pltpu.CompilerParams(vmem_limit_bytes=60 * 2**20),
    )(coef, field, pot)
    return coef, field.reshape(rs_field.shape), pot.reshape(potential.shape)


def solution(mesh):
    placed = (
        P(None, "row", "grp"),
        P("row", None, None, None),
        P("row", None),
        P(),
        P(),
        P(None, ("grp", "row"), None, None),
        P(None, ("grp", "row"), None, None),
    )
    return jax.shard_map(
        functools.partial(body, mesh.shape["grp"], mesh.shape["row"]),
        mesh=mesh,
        in_specs=placed,
        out_specs=(
            P(None, "row", "grp"),
            P(None, ("grp", "row"), None, None),
            P(None, ("grp", "row"), None, None),
        ),
        check_vma=False,
    )
```
